32 devices in a mesh: pts: 2 (over core), geo: 16 (over z, y, x).
Axes of the slice: x: 2, y: 2, z: 4, core: 2. Of those that a mesh axis runs over, the one named last changes fastest.
Arguments:
- points: bfloat16 [16, 1024, 256], P('geo', 'pts'), may hold values from -6 to 6
- result_grad: bfloat16 [16, 1024, 256], P('geo', 'pts'), may hold values from -6 to 6
- lists_one: int32 [16, 8, 4], P('geo', 'pts'), may hold values from 0 to 7, all different within a row
- lists_two: int32 [16, 8, 4], P('geo', 'pts'), may hold values from 0 to 7, all different within a row
- rotation: int32 [16, 1024], P('geo', 'pts'), may hold values from 0 to 1023, each once within a row
- gain_one: bfloat16 [256], replicated, may hold values from 0.25 to 1.75
- qkv_one: bfloat16 [256, 768], replicated, may hold values from -0.375 to 0.375
- out_one: bfloat16 [256, 256], replicated, may hold values from -0.375 to 0.375
- gain_two: bfloat16 [256], replicated, may hold values from 0.25 to 1.75
- qkv_two: bfloat16 [256, 768], replicated, may hold values from -0.375 to 0.375
- out_two: bfloat16 [256, 256], replicated, may hold values from -0.375 to 0.375
Outputs:
- result: bfloat16 [16, 1024, 256], P('geo', 'pts')
- points_grad: bfloat16 [16, 1024, 256], P('geo', 'pts')
- gain_one_grad: float32 [256], replicated
- qkv_one_grad: float32 [256, 768], replicated
- out_one_grad: float32 [256, 256], replicated
- gain_two_grad: float32 [256], replicated
- qkv_two_grad: float32 [256, 768], replicated
- out_two_grad: float32 [256, 256], replicated
The draws below stay inside these ranges and needn't reach their ends.
Inputs may be any that keep to these rules, and one draw needn't show every extreme that they name: `lists_one`: each ball lists 4 different balls of its geometry. `lists_two`: each ball lists 4 different balls of its geometry. `rotation`: each geometry's row is a permutation of its points.
All inputs are finite; a program needn't handle non-finite values.
Results may differ from the reference program's by a relative error of at most 0.012.
Values may be sent and summed in bfloat16 or wider, within the bound.
No kernel may reach another device: no remote copies, remote signals or barrier semaphores. Data moves between devices by JAX's collectives and lax.ppermute only.
A program may use at most 64 MiB of HBM per device.

```python
import jax
import jax.numpy as jnp
from jax import lax

D = 256
HEADS = 4
BALL = 128
LISTED = 4
POINTS = 1024
BALLS = 8
GEOS = 16


def steps_of(own_key, shape, shards, smallest, top_value):
    level = 1.0
    for position, parts in shards:
        heights = jax.random.uniform(jax.random.fold_in(jax.random.fold_in(own_key, 6), position), (parts,), jnp.float32, smallest / len(shards), top_value / len(shards))
        level = level * jnp.repeat(jnp.exp(heights), shape[position] // parts).reshape((-1,) + (1,) * (len(shape) - 1 - position))
    return level


def choose_distinct(rng, rows, number_of, top, lift):
    order = jax.random.permutation(jax.random.fold_in(rng, 1), number_of)
    favour = order
    for power in range(3):
        favour = favour * favour // number_of
    favour = favour * lift // number_of
    chance = jax.random.randint(jax.random.fold_in(rng, 2), (rows, number_of), 0, 4096) + favour
    fixed_rows = jax.random.permutation(jax.random.fold_in(rng, 3), rows)[jnp.arange(number_of) % rows]
    chance = jnp.where(jnp.arange(rows)[:, None] == fixed_rows[None, :], 1 << 14, chance)
    score = chance * number_of + jnp.arange(number_of)
    return lax.top_k(score.astype(jnp.int32), top)[1].astype(jnp.int32)


def scatter_about(rng, dims, deviation, most, split=(), dtype=jnp.bfloat16):
    array = deviation * jax.random.normal(rng, dims, jnp.float32)
    if split:
        array = array * steps_of(rng, dims, split, -0.22, 0.18)
    return jnp.clip(array, -most, most).astype(dtype)


def setup_inputs(seed: int = 0) -> dict:
    arg_keys = jax.random.split(jax.random.key(seed), 12)
    return {
        "points": scatter_about(arg_keys[0], (GEOS, POINTS, D), 1.0, 6.0, ((0, 16), (1, 2))),
        "result_grad": scatter_about(arg_keys[1], (GEOS, POINTS, D), 1.0, 6.0, ((0, 16), (1, 2))),
        "lists_one": choose_distinct(arg_keys[2], GEOS * BALLS, BALLS, LISTED, 0).reshape((GEOS, BALLS, LISTED)),
        "lists_two": choose_distinct(arg_keys[3], GEOS * BALLS, BALLS, LISTED, 0).reshape((GEOS, BALLS, LISTED)),
        "rotation": jax.vmap(lambda own: jax.random.permutation(own, POINTS))(jax.random.split(arg_keys[4], GEOS)).reshape((GEOS, POINTS)).astype(jnp.int32),
        "gain_one": jnp.clip(1.0 + 0.15 * jax.random.normal(arg_keys[5], (D,), jnp.float32), 0.25, 1.75).astype(jnp.bfloat16),
        "qkv_one": scatter_about(arg_keys[6], (D, 3 * D), D ** -0.5, 0.375),
        "out_one": scatter_about(arg_keys[7], (D, D), D ** -0.5, 0.375),
        "gain_two": jnp.clip(1.0 + 0.15 * jax.random.normal(arg_keys[8], (D,), jnp.float32), 0.25, 1.75).astype(jnp.bfloat16),
        "qkv_two": scatter_about(arg_keys[9], (D, 3 * D), D ** -0.5, 0.375),
        "out_two": scatter_about(arg_keys[10], (D, D), D ** -0.5, 0.375),
    }


HIGH = lax.Precision.HIGHEST

def pick_rows(source, indices):
    return jnp.take(source, indices, axis=0)

def keep_cotangent(values):
    rounded = values.astype(jnp.bfloat16).astype(jnp.float32)
    return lax.stop_gradient(rounded) + (values - lax.stop_gradient(values))

def round_cotangent(values):
    rounded = values.astype(jnp.bfloat16).astype(jnp.float32)
    return lax.stop_gradient(values) + (rounded - lax.stop_gradient(rounded))

def prepare(inputs, gain, weight):
    meansq = lax.optimization_barrier(jnp.mean(inputs * inputs, axis=-1, keepdims=True))
    normed = (inputs * lax.rsqrt(meansq + 1e-06) * gain).astype(jnp.bfloat16).astype(jnp.float32)
    projected = jnp.einsum('gnd,de->gne', normed, weight, precision=HIGH)
    width = inputs.shape[-1]
    return (projected[..., :width].astype(jnp.bfloat16), keep_cotangent(projected[..., width:]))

def attend(inputs, queries, keyvals, listed, weight):
    groups, rows, width = inputs.shape
    local_balls = rows // BALL
    head_dim = width // HEADS
    query_blocks = queries.astype(jnp.float32).reshape(groups, local_balls, BALL, HEADS, head_dim)
    blocks = keyvals.reshape(groups, -1, BALL, 2, HEADS, head_dim)
    chosen = jax.vmap(pick_rows)(blocks, listed)
    chosen = chosen.reshape(groups, local_balls, LISTED * BALL, 2, HEADS, head_dim)
    products = jnp.einsum('gbqhd,gbkhd->gbhqk', query_blocks, chosen[:, :, :, 0], precision=HIGH)
    scores = round_cotangent(products) * head_dim ** (-0.5)
    topmost = lax.stop_gradient(lax.optimization_barrier(jnp.max(scores, axis=-1, keepdims=True)))
    exponent = jnp.exp(scores - topmost)
    probs = exponent / lax.optimization_barrier(jnp.sum(exponent, axis=-1, keepdims=True))
    probs = probs.astype(jnp.bfloat16).astype(jnp.float32)
    mixed = jnp.einsum('gbhqk,gbkhd->gbqhd', probs, chosen[:, :, :, 1], precision=HIGH)
    mixed = mixed.astype(jnp.bfloat16).astype(jnp.float32).reshape(groups, rows, width)
    output = jnp.einsum('gnd,de->gne', mixed, weight, precision=HIGH)
    return (inputs + output).astype(jnp.bfloat16)

def layer(rows, listed, gain, weight_in, weight_out):
    inputs = rows.astype(jnp.float32)
    queries, keyvals = prepare(inputs, gain, weight_in)
    return attend(inputs, queries, keyvals, listed, weight_out)

def reference(points, result_grad, lists_one, lists_two, rotation, gain_one, qkv_one, out_one, gain_two, qkv_two, out_two):
    weights = tuple((item.astype(jnp.float32) for item in (gain_one, qkv_one, out_one, gain_two, qkv_two, out_two)))

    def model(inputs, params):

        def one_geometry(packed):
            rows, first, second, order = packed
            hidden = layer(rows[None], first[None], params[0], params[1], params[2])
            moved = jnp.take(hidden[0], order, axis=0)[None]
            return layer(moved, second[None], params[3], params[4], params[5])[0]
        return lax.map(jax.checkpoint(one_geometry), (inputs, lists_one, lists_two, rotation))
    result, backward = jax.vjp(model, points, weights)
    points_grad, grads = backward(result_grad)
    return (result, points_grad, grads[0], grads[1], grads[2], grads[3], grads[4], grads[5])
```

```python
import functools

import jax
import jax.numpy as jnp
from jax import lax
from jax.experimental import pallas as pl
from jax.experimental.pallas import tpu as pltpu
from jax.sharding import PartitionSpec as P

HEADS = 4
BALL = 128
LISTED = 4
EPSILON = 1e-06
BF = jnp.bfloat16
F32 = jnp.float32
SWAP = ((0, 1), (1, 0))
PIECES = 4

VMEM = pl.BlockSpec(memory_space=pltpu.VMEM)
SMEM = pl.BlockSpec(memory_space=pltpu.SMEM)
PARAMS = pltpu.CompilerParams(vmem_limit_bytes=40 * 1024 * 1024)


def dot(a, b, dims=((1,), (0,))):
    return lax.dot_general(a, b, (dims, ((), ())), preferred_element_type=F32)


def norm_factor(x):
    return lax.rsqrt(jnp.mean(x * x, axis=-1, keepdims=True) + EPSILON)


def own_columns(weight, core, half):
    width = weight.shape[0]
    return [weight[:, pl.ds(pl.multiple_of(i * width + core * half, half), half)] for i in range(3)]


def project(normed, columns):
    qkv = dot(normed, jnp.concatenate(columns, axis=1))
    half = columns[0].shape[1]
    scale = (2 * half // HEADS) ** (-0.5)
    return qkv[:, :half].astype(BF) * BF(scale), qkv[:, half:].astype(BF)


def stack_heads(rows):
    lane = lax.broadcasted_iota(jnp.int32, rows.shape, 1)
    first = lane < rows.shape[1] // 2
    zero = jnp.zeros_like(rows)
    return jnp.concatenate([jnp.where(first, rows, zero), jnp.where(first, zero, rows)], axis=0)


def unstack_heads(stacked):
    rows = stacked.shape[0] // 2
    lane = lax.broadcasted_iota(jnp.int32, (rows, stacked.shape[1]), 1)
    return jnp.where(lane < stacked.shape[1] // 2, stacked[:rows], stacked[rows:])


def listed_balls(ball, mine, other, core, offset, local_balls):
    base = offset + lax.rem(ball, local_balls) * LISTED
    is_mine = ball // local_balls == core
    return [jnp.where(is_mine, mine[base + j], other[base + j]) for j in range(LISTED)]


def rows_of(ball):
    return pl.ds(pl.multiple_of(ball * BALL, BALL), BALL)


def pick(ref, listed, first, half):
    return jnp.concatenate([ref[rows_of(i), first : first + half] for i in listed], axis=0)


def softmax_parts(stacked, keys):
    scores = dot(stacked, keys, ((1,), (1,)))
    exponent = jnp.exp(scores - jnp.max(scores, axis=-1, keepdims=True))
    return exponent, 1.0 / jnp.sum(exponent, axis=-1, keepdims=True)


def mix(exponent, inverse, values):
    return unstack_heads(dot(exponent.astype(BF), values) * inverse)


def ball_backward(stacked, keys, values, exponent, inverse, mixed, mixed_grad):
    grad = stack_heads(mixed_grad.astype(F32)) * inverse
    inner = jnp.sum(grad * jnp.concatenate([mixed, mixed], axis=0), axis=-1, keepdims=True)
    grad = grad.astype(BF)
    scores_grad = (exponent * (dot(grad, values, ((1,), (1,))) - inner)).astype(BF)
    scale = (stacked.shape[1] // 2) ** (-0.5)
    queries_grad = unstack_heads(dot(scores_grad, keys)) * scale
    keys_grad = dot(stacked, scores_grad, ((0,), (0,)))
    values_grad = dot(grad, exponent.astype(BF), ((0,), (0,)))
    return queries_grad.astype(BF), keys_grad, values_grad


def add_listed(ref, listed, part):
    for j, i in enumerate(listed):
        ref[i] += part[:, j * BALL : (j + 1) * BALL]


def qkv_grads(dq, dk_ref, dv_ref):
    balls = dk_ref.shape[0]
    parts = [dq]
    for ref in (dk_ref, dv_ref):
        parts.append(jnp.concatenate([ref[i].T for i in range(balls)], axis=0).astype(BF))
    return jnp.concatenate(parts, axis=1)


def store_pieces(ref, pieces, slot_bits):
    for p, piece in enumerate(pieces):
        ref[p ^ slot_bits] = piece.astype(BF)


def weight_pieces(normed, grads, mixed, grad_out):
    half = mixed.shape[1]
    weight = dot(normed, grads, ((0,), (0,)))
    out = dot(mixed, grad_out, ((0,), (0,)))
    pieces = [weight[:, i * half : (i + 1) * half] for i in range(3)]
    return pieces + [jnp.concatenate([out[:, :half], out[:, half:]], axis=0)]


def norm_backward(normed_grad, x, gain, grad_out):
    factor = norm_factor(x)
    scaled = normed_grad.astype(BF).astype(F32) * gain
    inner = jnp.mean(scaled * x, axis=-1, keepdims=True)
    return (grad_out.astype(F32) + factor * scaled - x * (factor * factor * factor) * inner).astype(BF)


def slot_bits():
    return lax.rem(lax.axis_index("geo"), PIECES)


def first_forward(mine, other, x_mine, x_other, gain, weight, mixed_ref, q_ref, kv_ref, normed_ref):
    core = lax.axis_index("pts")
    local, width = x_mine.shape
    half = width // 2
    columns = own_columns(weight, core, half)
    scaled_gain = gain[...].astype(F32)
    for place, ref in ((core, x_mine), (1 - core, x_other)):
        x = ref[...].astype(F32)
        normed = (x * norm_factor(x) * scaled_gain).astype(BF)
        rows = pl.ds(pl.multiple_of(place * local, local), local)
        normed_ref[rows, :] = normed
        q_ref[rows, :], kv_ref[rows, :] = project(normed, columns)

    def one_ball(ball, carry):
        listed = listed_balls(ball, mine, other, core, 0, local // BALL)
        stacked = stack_heads(q_ref[rows_of(ball), :])
        exponent, inverse = softmax_parts(stacked, pick(kv_ref, listed, 0, half))
        mixed = mix(exponent, inverse, pick(kv_ref, listed, half, half))
        mixed_ref[rows_of(ball), :] = mixed.astype(BF)
        return carry

    lax.fori_loop(0, 2 * local // BALL, one_ball, 0)


def second_layer(
    mine, other, rot_mine, rot_other, x_mine, x_other, mixed_mine, mixed_other, grad_mine, grad_other,
    out_one, gain, weight, out_two,
    moved_ref, mixed_ref, part_ref, pieces_ref,
    both_ref, hidden_ref, grad_ref, normed_ref, q_ref, kv_ref, mg_ref, dq_ref, dk_ref, dv_ref,
):
    core = lax.axis_index("pts")
    local, width = x_mine.shape
    half = width // 2
    total = 2 * local

    def lanes(place):
        return pl.ds(pl.multiple_of(place * half, half), half)

    def rows(place):
        return pl.ds(pl.multiple_of(place * local, local), local)

    both_ref[:, lanes(core)] = mixed_mine[...]
    both_ref[:, lanes(1 - core)] = mixed_other[...]
    for place, ref, grad in ((core, x_mine, grad_mine), (1 - core, x_other, grad_other)):
        out = dot(both_ref[rows(place), :], out_one[...])
        hidden_ref[rows(place), :] = (ref[...].astype(F32) + out).astype(BF)
        grad_ref[rows(place), :] = grad[...]
    hidden = hidden_ref[...]
    columns = own_columns(weight, core, half)
    scaled_gain = gain[...].astype(F32)
    lane = lax.broadcasted_iota(jnp.int32, (BALL, total), 1).astype(F32)
    for place, ref in ((core, rot_mine), (1 - core, rot_other)):
        for j in range(local // BALL):
            row = ref[j : j + 1, :].astype(F32)
            column = jnp.broadcast_to(row, (BALL, BALL)).T[:, :1]
            moved = dot((lane == column).astype(BF), hidden)
            at = pl.ds(pl.multiple_of(place * local + j * BALL, BALL), BALL)
            normed = (moved * norm_factor(moved) * scaled_gain).astype(BF)
            moved_ref[at, :] = moved.astype(BF)
            normed_ref[at, :] = normed
    q_ref[...], kv_ref[...] = project(normed_ref[...], columns)
    out_columns = out_two[pl.ds(pl.multiple_of(core * half, half), half), :]
    mg_ref[...] = dot(grad_ref[...], out_columns, ((1,), (1,))).astype(BF)
    dk_ref[...] = jnp.zeros_like(dk_ref)
    dv_ref[...] = jnp.zeros_like(dv_ref)

    def one_ball(ball, carry):
        listed = listed_balls(ball, mine, other, core, (local // BALL) * LISTED, local // BALL)
        at = rows_of(ball)
        stacked = stack_heads(q_ref[at, :])
        keys = pick(kv_ref, listed, 0, half)
        values = pick(kv_ref, listed, half, half)
        exponent, inverse = softmax_parts(stacked, keys)
        mixed = mix(exponent, inverse, values)
        mixed_ref[at, :] = mixed.astype(BF)
        dq, dk, dv = ball_backward(stacked, keys, values, exponent, inverse, mixed, mg_ref[at, :])
        dq_ref[at, :] = dq
        add_listed(dk_ref, listed, dk)
        add_listed(dv_ref, listed, dv)
        return carry

    lax.fori_loop(0, total // BALL, one_ball, 0)
    grads = qkv_grads(dq_ref[...], dk_ref, dv_ref)
    part_ref[...] = dot(grads, jnp.concatenate(columns, axis=1), ((1,), (1,))).astype(BF)
    store_pieces(pieces_ref, weight_pieces(normed_ref[...], grads, mixed_ref[...], grad_ref[...]), slot_bits())


def first_backward(
    mine, other, rot_mine, rot_other, part_mine, part_other, moved_ref, grad_mine, grad_other, gain_two,
    mixed_ref, normed_ref, q_ref, kv_ref, weight, out_one, pieces_two,
    keep_ref, send_ref, part_keep, part_send, hidden_grad_mine,
    rows_grad_ref, hg_ref, mg_ref, dq_ref, dk_ref, dv_ref, pieces_ref,
):
    core = lax.axis_index("pts")
    local, width = grad_mine.shape
    half = width // 2
    total = 2 * local

    def rows(place):
        return pl.ds(pl.multiple_of(place * local, local), local)

    gain = gain_two[...].astype(F32)
    for place, grad in ((core, grad_mine), (1 - core, grad_other)):
        normed_grad = part_mine[rows(place), :].astype(F32) + part_other[rows(place), :].astype(F32)
        x = moved_ref[rows(place), :].astype(F32)
        rows_grad_ref[rows(place), :] = norm_backward(normed_grad, x, gain, grad[...])

    place_of = jnp.where(core == 0, rot_mine[: local // BALL, :], rot_other[: local // BALL, :])
    place_of_high = jnp.where(core == 0, rot_other[: local // BALL, :], rot_mine[: local // BALL, :])
    row_of = [place_of[j : j + 1, :] for j in range(local // BALL)]
    row_of += [place_of_high[j : j + 1, :] for j in range(local // BALL)]
    order = jnp.concatenate(row_of, axis=1).astype(F32)
    rows_grad = rows_grad_ref[...]
    sub = lax.broadcasted_iota(jnp.int32, (BALL, total), 0).astype(F32)
    out_rows = out_one[pl.ds(pl.multiple_of(core * half, half), half), :]
    for j in range(total // BALL):
        chosen = (sub + float(j * BALL) == order).astype(BF)
        hg_ref[j * BALL : (j + 1) * BALL, :] = dot(chosen, rows_grad).astype(BF)
    hidden_grad = hg_ref[...]
    hidden_grad_mine[...] = hg_ref[rows(core), :]
    mg_ref[...] = dot(hidden_grad, out_rows, ((1,), (1,))).astype(BF)
    dk_ref[...] = jnp.zeros_like(dk_ref)
    dv_ref[...] = jnp.zeros_like(dv_ref)

    def one_ball(ball, carry):
        listed = listed_balls(ball, mine, other, core, 0, local // BALL)
        at = rows_of(ball)
        stacked = stack_heads(q_ref[at, :])
        keys = pick(kv_ref, listed, 0, half)
        values = pick(kv_ref, listed, half, half)
        exponent, inverse = softmax_parts(stacked, keys)
        mixed = mixed_ref[at, :].astype(F32)
        dq, dk, dv = ball_backward(stacked, keys, values, exponent, inverse, mixed, mg_ref[at, :])
        dq_ref[at, :] = dq
        add_listed(dk_ref, listed, dk)
        add_listed(dv_ref, listed, dv)
        return carry

    lax.fori_loop(0, total // BALL, one_ball, 0)
    grads = qkv_grads(dq_ref[...], dk_ref, dv_ref)
    columns = jnp.concatenate(own_columns(weight, core, half), axis=1)
    store_pieces(pieces_ref, weight_pieces(normed_ref[...], grads, mixed_ref[...], hidden_grad), slot_bits())
    for slot in range(PIECES // 2):
        keep_ref[slot, 0] = pieces_ref[slot]
        keep_ref[slot, 1] = pieces_two[slot]
        send_ref[slot, 0] = pieces_ref[slot + PIECES // 2]
        send_ref[slot, 1] = pieces_two[slot + PIECES // 2]
    part = dot(grads, columns, ((1,), (1,)))
    hg_ref[...] = part.astype(BF)
    part_keep[...] = hg_ref[rows(core), :]
    part_send[...] = hg_ref[rows(1 - core), :]


def finish_rows(
    part_mine, part_other, x_mine, gain, hidden_grad, moved, mixed_mine, mixed_other, out_two,
    points_grad, result, both_ref,
):
    core = lax.axis_index("pts")
    local, width = x_mine.shape
    half = width // 2
    normed_grad = part_mine[...].astype(F32) + part_other[...].astype(F32)
    points_grad[...] = norm_backward(
        normed_grad, x_mine[...].astype(F32), gain[...].astype(F32), hidden_grad[...]
    )
    rows = pl.ds(pl.multiple_of(core * local, local), local)
    both_ref[:, pl.ds(pl.multiple_of(core * half, half), half)] = mixed_mine[rows, :]
    both_ref[:, pl.ds(pl.multiple_of((1 - core) * half, half), half)] = mixed_other[...]
    out = dot(both_ref[...], out_two[...])
    result[...] = (moved[rows, :].astype(F32) + out).astype(BF)


def finish_weights(
    near_mine, far_mine, near_other, far_other, gain_one, gain_two, weight_one, weight_two,
    gain_one_grad, qkv_one_grad, out_one_grad, gain_two_grad, qkv_two_grad, out_two_grad,
    slots_ref,
):
    core = lax.axis_index("pts")
    half = near_mine.shape[-1]
    width = 2 * half
    mask = slot_bits()
    groups = ((core, near_mine, far_mine), (1 - core, near_other, far_other))
    for side, (_, near, far) in enumerate(groups):
        for slot in range(PIECES // 2):
            slots_ref[side, slot] = near[slot]
            slots_ref[side, slot + PIECES // 2] = far[slot]
    layers = (
        (gain_one, weight_one, gain_one_grad, qkv_one_grad, out_one_grad),
        (gain_two, weight_two, gain_two_grad, qkv_two_grad, out_two_grad),
    )
    for layer, (gain, weight, gain_grad, qkv_grad, out_grad) in enumerate(layers):
        folded = jnp.zeros((width, half), F32)
        for side, (place, _, _) in enumerate(groups):
            for p in range(3):
                piece = slots_ref[side, p ^ mask, layer].astype(F32)
                at = pl.ds(pl.multiple_of(p * width + place * half, half), half)
                qkv_grad[:, at] = piece
                folded = folded + piece * weight[:, at].astype(F32)
            piece = slots_ref[side, 3 ^ mask, layer].astype(F32)
            at = pl.ds(pl.multiple_of(place * half, half), half)
            out_grad[at, :half] = piece[:half]
            out_grad[at, half:] = piece[half:]
        gain_grad[...] = jnp.sum(folded.T, axis=0, keepdims=True) / gain[...].astype(F32)


def shape(dims, dtype=BF):
    return jax.ShapeDtypeStruct(dims, dtype)


def call(body, name, ins, outs, scratch=()):
    specs = [SMEM if kind == "s" else VMEM for kind, _ in ins]
    return pl.pallas_call(
        body,
        name=name,
        out_shape=outs,
        in_specs=specs,
        out_specs=[VMEM] * len(outs),
        scratch_shapes=[pltpu.VMEM(dims, dtype) for dims, dtype in scratch],
        compiler_params=PARAMS,
    )(*[array for _, array in ins])


def add(a, b):
    return (a.astype(F32) + b.astype(F32)).astype(BF)


def local(
    geo,
    points,
    result_grad,
    lists_one,
    lists_two,
    rotation,
    gain_one,
    qkv_one,
    out_one,
    gain_two,
    qkv_two,
    out_two,
):
    rows, width = points.shape[1:]
    half = width // 2
    total = 2 * rows
    balls = total // BALL

    def swap(array):
        return lax.ppermute(array, "pts", SWAP)

    def across(array, bit):
        return lax.ppermute(array, "geo", [(i, i ^ bit) for i in range(geo)])

    x = points[0]
    grad = result_grad[0]
    lists = jnp.concatenate([lists_one.reshape(-1), lists_two.reshape(-1)])
    rot = rotation.reshape(rows // BALL, BALL)
    x_other = swap(x)
    lists_other = swap(lists)
    grad_other = swap(grad)
    rot_other = swap(rot)
    gain_one = gain_one.reshape(1, width)
    gain_two = gain_two.reshape(1, width)

    mixed, q, kv, normed = call(
        first_forward,
        "first_forward",
        [("s", lists), ("s", lists_other)] + [("v", a) for a in (x, x_other, gain_one, qkv_one)],
        [shape((total, half)), shape((total, half)), shape((total, width)), shape((total, width))],
    )
    mixed_other = swap(mixed)
    blocks = ((balls, half, BALL), F32)
    moved, mixed_two, part_two, pieces_two = call(
        second_layer,
        "second_layer",
        [("s", lists), ("s", lists_other)]
        + [
            ("v", a)
            for a in (
                rot, rot_other, x, x_other, mixed, mixed_other, grad, grad_other, out_one, gain_two, qkv_two, out_two
            )
        ],
        [shape((total, width)), shape((total, half)), shape((total, width)), shape((PIECES, width, half))],
        [
            ((total, width), BF),
            ((total, width), BF),
            ((total, width), BF),
            ((total, width), BF),
            ((total, half), BF),
            ((total, width), BF),
            ((total, half), BF),
            ((total, half), BF),
            blocks,
            blocks,
        ],
    )
    part_two_other = swap(part_two)
    core = lax.axis_index("pts")
    mixed_two_other = swap(lax.dynamic_slice_in_dim(mixed_two, (1 - core) * rows, rows, 0))
    keep, send, part_keep, part_send, hidden_grad = call(
        first_backward,
        "first_backward",
        [("s", lists), ("s", lists_other)]
        + [
            ("v", a)
            for a in (
                rot, rot_other, part_two, part_two_other, moved, grad, grad_other, gain_two,
                mixed, normed, q, kv, qkv_one, out_one, pieces_two,
            )
        ],
        [shape((PIECES // 2, 2, width, half))] * 2 + [shape((rows, width))] * 3,
        [
            ((total, width), BF),
            ((total, width), BF),
            ((total, half), BF),
            ((total, half), BF),
            blocks,
            blocks,
            ((PIECES, width, half), BF),
        ],
    )
    part_other = swap(part_send)
    summed = add(keep, across(send, 2))
    summed = add(summed[:1], across(summed[1:], 1))
    bit = PIECES
    while bit < geo:
        summed = add(summed, across(summed, bit))
        bit *= 2
    near = jnp.concatenate([summed, across(summed, 1)], axis=0)
    far = across(near, 2)
    near_other = swap(near)
    far_other = swap(far)
    points_grad, result = call(
        finish_rows,
        "finish_rows",
        [
            ("v", a)
            for a in (part_keep, part_other, x, gain_one, hidden_grad, moved, mixed_two, mixed_two_other, out_two)
        ],
        [shape((rows, width))] * 2,
        [((rows, width), BF)],
    )
    vector, matrix, square = (shape(dims, F32) for dims in ((1, width), (width, 3 * width), (width, width)))
    grads = call(
        finish_weights,
        "finish_weights",
        [("v", a) for a in (near, far, near_other, far_other, gain_one, gain_two, qkv_one, qkv_two)],
        [vector, matrix, square] * 2,
        [((2, PIECES, 2, width, half), BF)],
    )
    return (
        result[None],
        points_grad[None],
        grads[0].reshape(width),
        grads[1],
        grads[2],
        grads[3].reshape(width),
        grads[4],
        grads[5],
    )


def solution(mesh):
    rows = P("geo", "pts", None)
    placed = (rows,) * 4 + (P("geo", "pts"),) + (P(),) * 6
    return jax.shard_map(
        functools.partial(local, mesh.shape["geo"]),
        mesh=mesh,
        in_specs=placed,
        out_specs=(rows, rows) + (P(),) * 6,
        check_vma=False,
    )
```

```python
import functools

import jax
import jax.numpy as jnp
from jax import lax
from jax.experimental import pallas as pl
from jax.experimental.pallas import tpu as pltpu
from jax.sharding import PartitionSpec as P

HEADS = 4
BALL = 128
LISTED = 4
EPSILON = 1e-06
BF = jnp.bfloat16
F32 = jnp.float32
SWAP = ((0, 1), (1, 0))
PIECES = 4

VMEM = pl.BlockSpec(memory_space=pltpu.VMEM)
SMEM = pl.BlockSpec(memory_space=pltpu.SMEM)
PARAMS = pltpu.CompilerParams(vmem_limit_bytes=40 * 1024 * 1024)


def dot(a, b, dims=((1,), (0,))):
    return lax.dot_general(a, b, (dims, ((), ())), preferred_element_type=F32)


def norm_factor(x):
    return lax.rsqrt(jnp.mean(x * x, axis=-1, keepdims=True) + EPSILON)


def own_columns(weight, core, half):
    width = weight.shape[0]
    return [weight[:, pl.ds(pl.multiple_of(i * width + core * half, half), half)] for i in range(3)]


def project(normed, columns):
    qkv = dot(normed, jnp.concatenate(columns, axis=1))
    half = columns[0].shape[1]
    scale = (2 * half // HEADS) ** (-0.5)
    return qkv[:, :half].astype(BF) * BF(scale), qkv[:, half:].astype(BF)


def stack_heads(rows):
    lane = lax.broadcasted_iota(jnp.int32, rows.shape, 1)
    first = lane < rows.shape[1] // 2
    zero = jnp.zeros_like(rows)
    return jnp.concatenate([jnp.where(first, rows, zero), jnp.where(first, zero, rows)], axis=0)


def unstack_heads(stacked):
    rows = stacked.shape[0] // 2
    lane = lax.broadcasted_iota(jnp.int32, (rows, stacked.shape[1]), 1)
    return jnp.where(lane < stacked.shape[1] // 2, stacked[:rows], stacked[rows:])


def listed_balls(ball, mine, other, core, offset, local_balls):
    base = offset + lax.rem(ball, local_balls) * LISTED
    is_mine = ball // local_balls == core
    return [jnp.where(is_mine, mine[base + j], other[base + j]) for j in range(LISTED)]


def rows_of(ball):
    return pl.ds(pl.multiple_of(ball * BALL, BALL), BALL)


def pick(ref, listed, first, half):
    return jnp.concatenate([ref[rows_of(i), first : first + half] for i in listed], axis=0)


def softmax_parts(stacked, keys):
    scores = dot(stacked, keys, ((1,), (1,)))
    exponent = jnp.exp(scores - jnp.max(scores, axis=-1, keepdims=True))
    return exponent, 1.0 / jnp.sum(exponent, axis=-1, keepdims=True)


def mix(exponent, inverse, values):
    return unstack_heads(dot(exponent.astype(BF), values) * inverse)


def ball_backward(stacked, keys, values, exponent, inverse, mixed, mixed_grad):
    grad = stack_heads(mixed_grad.astype(F32)) * inverse
    inner = jnp.sum(grad * jnp.concatenate([mixed, mixed], axis=0), axis=-1, keepdims=True)
    grad = grad.astype(BF)
    scores_grad = (exponent * (dot(grad, values, ((1,), (1,))) - inner)).astype(BF)
    scale = (stacked.shape[1] // 2) ** (-0.5)
    queries_grad = unstack_heads(dot(scores_grad, keys)) * scale
    keys_grad = dot(stacked, scores_grad, ((0,), (0,)))
    values_grad = dot(grad, exponent.astype(BF), ((0,), (0,)))
    return queries_grad.astype(BF), keys_grad, values_grad


def add_listed(ref, listed, part):
    for j, i in enumerate(listed):
        ref[i] += part[:, j * BALL : (j + 1) * BALL]


def qkv_grads(dq, dk_ref, dv_ref):
    balls = dk_ref.shape[0]
    parts = [dq]
    for ref in (dk_ref, dv_ref):
        parts.append(jnp.concatenate([ref[i].T for i in range(balls)], axis=0).astype(BF))
    return jnp.concatenate(parts, axis=1)


def store_pieces(ref, keep_ref, send_ref, pieces, core):
    mask = slot_mask(core)
    for p, piece in enumerate(pieces):
        ref[p ^ mask] = piece.astype(BF)
    keep_ref[...] = ref[: PIECES // 2]
    send_ref[...] = ref[PIECES // 2 :]


def weight_pieces(normed, grads, mixed, grad_out):
    half = mixed.shape[1]
    weight = dot(normed, grads, ((0,), (0,)))
    out = dot(mixed, grad_out, ((0,), (0,)))
    pieces = [weight[:, i * half : (i + 1) * half] for i in range(3)]
    return pieces + [jnp.concatenate([out[:, :half], out[:, half:]], axis=0)]


def norm_backward(normed_grad, x, gain, grad_out):
    factor = norm_factor(x)
    scaled = normed_grad.astype(BF).astype(F32) * gain
    inner = jnp.mean(scaled * x, axis=-1, keepdims=True)
    return (grad_out.astype(F32) + factor * scaled - x * (factor * factor * factor) * inner).astype(BF)


def slot_mask(core):
    low = lax.rem(lax.axis_index("geo"), PIECES)
    return jnp.where(core == 0, low, (low & 1) * 2 + low // 2)


def first_forward(mine, other, x_mine, x_other, gain, weight, mixed_ref, q_ref, kv_ref, normed_ref):
    core = lax.axis_index("pts")
    local, width = x_mine.shape
    half = width // 2
    columns = own_columns(weight, core, half)
    scaled_gain = gain[...].astype(F32)
    for place, ref in ((core, x_mine), (1 - core, x_other)):
        x = ref[...].astype(F32)
        normed = (x * norm_factor(x) * scaled_gain).astype(BF)
        rows = pl.ds(pl.multiple_of(place * local, local), local)
        normed_ref[rows, :] = normed
        q_ref[rows, :], kv_ref[rows, :] = project(normed, columns)

    def one_ball(ball, carry):
        listed = listed_balls(ball, mine, other, core, 0, local // BALL)
        stacked = stack_heads(q_ref[rows_of(ball), :])
        exponent, inverse = softmax_parts(stacked, pick(kv_ref, listed, 0, half))
        mixed = mix(exponent, inverse, pick(kv_ref, listed, half, half))
        mixed_ref[rows_of(ball), :] = mixed.astype(BF)
        return carry

    lax.fori_loop(0, 2 * local // BALL, one_ball, 0)


def second_layer(
    mine, other, rot_mine, rot_other, x_mine, x_other, mixed_mine, mixed_other, grad_mine, grad_other,
    out_one, gain, weight, out_two,
    moved_ref, mixed_ref, part_ref, keep_ref, send_ref,
    both_ref, hidden_ref, grad_ref, normed_ref, q_ref, kv_ref, mg_ref, dq_ref, dk_ref, dv_ref, pieces_ref,
):
    core = lax.axis_index("pts")
    local, width = x_mine.shape
    half = width // 2
    total = 2 * local

    def lanes(place):
        return pl.ds(pl.multiple_of(place * half, half), half)

    def rows(place):
        return pl.ds(pl.multiple_of(place * local, local), local)

    both_ref[:, lanes(core)] = mixed_mine[...]
    both_ref[:, lanes(1 - core)] = mixed_other[...]
    for place, ref, grad in ((core, x_mine, grad_mine), (1 - core, x_other, grad_other)):
        out = dot(both_ref[rows(place), :], out_one[...])
        hidden_ref[rows(place), :] = (ref[...].astype(F32) + out).astype(BF)
        grad_ref[rows(place), :] = grad[...]
    hidden = hidden_ref[...]
    columns = own_columns(weight, core, half)
    scaled_gain = gain[...].astype(F32)
    lane = lax.broadcasted_iota(jnp.int32, (BALL, total), 1).astype(F32)
    for place, ref in ((core, rot_mine), (1 - core, rot_other)):
        for j in range(local // BALL):
            row = ref[j : j + 1, :].astype(F32)
            column = jnp.broadcast_to(row, (BALL, BALL)).T[:, :1]
            moved = dot((lane == column).astype(BF), hidden)
            at = pl.ds(pl.multiple_of(place * local + j * BALL, BALL), BALL)
            normed = (moved * norm_factor(moved) * scaled_gain).astype(BF)
            moved_ref[at, :] = moved.astype(BF)
            normed_ref[at, :] = normed
    q_ref[...], kv_ref[...] = project(normed_ref[...], columns)
    out_columns = out_two[pl.ds(pl.multiple_of(core * half, half), half), :]
    mg_ref[...] = dot(grad_ref[...], out_columns, ((1,), (1,))).astype(BF)
    dk_ref[...] = jnp.zeros_like(dk_ref)
    dv_ref[...] = jnp.zeros_like(dv_ref)

    def one_ball(ball, carry):
        listed = listed_balls(ball, mine, other, core, (local // BALL) * LISTED, local // BALL)
        at = rows_of(ball)
        stacked = stack_heads(q_ref[at, :])
        keys = pick(kv_ref, listed, 0, half)
        values = pick(kv_ref, listed, half, half)
        exponent, inverse = softmax_parts(stacked, keys)
        mixed = mix(exponent, inverse, values)
        mixed_ref[at, :] = mixed.astype(BF)
        dq, dk, dv = ball_backward(stacked, keys, values, exponent, inverse, mixed, mg_ref[at, :])
        dq_ref[at, :] = dq
        add_listed(dk_ref, listed, dk)
        add_listed(dv_ref, listed, dv)
        return carry

    lax.fori_loop(0, total // BALL, one_ball, 0)
    grads = qkv_grads(dq_ref[...], dk_ref, dv_ref)
    part_ref[...] = dot(grads, jnp.concatenate(columns, axis=1), ((1,), (1,))).astype(BF)
    pieces = weight_pieces(normed_ref[...], grads, mixed_ref[...], grad_ref[...])
    store_pieces(pieces_ref, keep_ref, send_ref, pieces, core)


def first_backward(
    mine, other, rot_mine, rot_other, part_mine, part_other, moved_ref, grad_mine, grad_other, gain_two,
    mixed_ref, normed_ref, q_ref, kv_ref, weight, out_one,
    keep_ref, send_ref, part_keep, part_send, hidden_grad_mine,
    rows_grad_ref, hg_ref, mg_ref, dq_ref, dk_ref, dv_ref, pieces_ref,
):
    core = lax.axis_index("pts")
    local, width = grad_mine.shape
    half = width // 2
    total = 2 * local

    def rows(place):
        return pl.ds(pl.multiple_of(place * local, local), local)

    gain = gain_two[...].astype(F32)
    for place, grad in ((core, grad_mine), (1 - core, grad_other)):
        normed_grad = part_mine[rows(place), :].astype(F32) + part_other[rows(place), :].astype(F32)
        x = moved_ref[rows(place), :].astype(F32)
        rows_grad_ref[rows(place), :] = norm_backward(normed_grad, x, gain, grad[...])

    place_of = jnp.where(core == 0, rot_mine[: local // BALL, :], rot_other[: local // BALL, :])
    place_of_high = jnp.where(core == 0, rot_other[: local // BALL, :], rot_mine[: local // BALL, :])
    row_of = [place_of[j : j + 1, :] for j in range(local // BALL)]
    row_of += [place_of_high[j : j + 1, :] for j in range(local // BALL)]
    order = jnp.concatenate(row_of, axis=1).astype(F32)
    rows_grad = rows_grad_ref[...]
    sub = lax.broadcasted_iota(jnp.int32, (BALL, total), 0).astype(F32)
    out_rows = out_one[pl.ds(pl.multiple_of(core * half, half), half), :]
    for j in range(total // BALL):
        chosen = (sub + float(j * BALL) == order).astype(BF)
        hg_ref[j * BALL : (j + 1) * BALL, :] = dot(chosen, rows_grad).astype(BF)
    hidden_grad = hg_ref[...]
    hidden_grad_mine[...] = hg_ref[rows(core), :]
    mg_ref[...] = dot(hidden_grad, out_rows, ((1,), (1,))).astype(BF)
    dk_ref[...] = jnp.zeros_like(dk_ref)
    dv_ref[...] = jnp.zeros_like(dv_ref)

    def one_ball(ball, carry):
        listed = listed_balls(ball, mine, other, core, 0, local // BALL)
        at = rows_of(ball)
        stacked = stack_heads(q_ref[at, :])
        keys = pick(kv_ref, listed, 0, half)
        values = pick(kv_ref, listed, half, half)
        exponent, inverse = softmax_parts(stacked, keys)
        mixed = mixed_ref[at, :].astype(F32)
        dq, dk, dv = ball_backward(stacked, keys, values, exponent, inverse, mixed, mg_ref[at, :])
        dq_ref[at, :] = dq
        add_listed(dk_ref, listed, dk)
        add_listed(dv_ref, listed, dv)
        return carry

    lax.fori_loop(0, total // BALL, one_ball, 0)
    grads = qkv_grads(dq_ref[...], dk_ref, dv_ref)
    columns = jnp.concatenate(own_columns(weight, core, half), axis=1)
    pieces = weight_pieces(normed_ref[...], grads, mixed_ref[...], hidden_grad)
    store_pieces(pieces_ref, keep_ref, send_ref, pieces, core)
    part = dot(grads, columns, ((1,), (1,)))
    hg_ref[...] = part.astype(BF)
    part_keep[...] = hg_ref[rows(core), :]
    part_send[...] = hg_ref[rows(1 - core), :]


def finish_rows(
    part_mine, part_other, x_mine, gain, hidden_grad, moved, mixed_mine, mixed_other, out_two,
    points_grad, result, both_ref,
):
    core = lax.axis_index("pts")
    local, width = x_mine.shape
    half = width // 2
    normed_grad = part_mine[...].astype(F32) + part_other[...].astype(F32)
    points_grad[...] = norm_backward(
        normed_grad, x_mine[...].astype(F32), gain[...].astype(F32), hidden_grad[...]
    )
    rows = pl.ds(pl.multiple_of(core * local, local), local)
    both_ref[:, pl.ds(pl.multiple_of(core * half, half), half)] = mixed_mine[rows, :]
    both_ref[:, pl.ds(pl.multiple_of((1 - core) * half, half), half)] = mixed_other[...]
    out = dot(both_ref[...], out_two[...])
    result[...] = (moved[rows, :].astype(F32) + out).astype(BF)


def finish_weights(
    near_mine, far_mine, near_other, far_other, gain, weight, gain_grad, qkv_grad, out_grad, slots_ref
):
    core = lax.axis_index("pts")
    half = near_mine.shape[-1]
    width = 2 * half
    groups = ((core, near_mine, far_mine), (1 - core, near_other, far_other))
    folded = jnp.zeros((width, half), F32)
    for side, (place, near, far) in enumerate(groups):
        slots_ref[side, : PIECES // 2] = near[...]
        slots_ref[side, PIECES // 2 :] = far[...]
        mask = slot_mask(place)
        for p in range(3):
            piece = slots_ref[side, p ^ mask].astype(F32)
            at = pl.ds(pl.multiple_of(p * width + place * half, half), half)
            qkv_grad[:, at] = piece
            folded = folded + piece * weight[:, at].astype(F32)
        piece = slots_ref[side, 3 ^ mask].astype(F32)
        at = pl.ds(pl.multiple_of(place * half, half), half)
        out_grad[at, :half] = piece[:half]
        out_grad[at, half:] = piece[half:]
    gain_grad[...] = jnp.sum(folded.T, axis=0, keepdims=True) / gain[...].astype(F32)


def shape(dims, dtype=BF):
    return jax.ShapeDtypeStruct(dims, dtype)


def call(body, name, ins, outs, scratch=()):
    specs = [SMEM if kind == "s" else VMEM for kind, _ in ins]
    return pl.pallas_call(
        body,
        name=name,
        out_shape=outs,
        in_specs=specs,
        out_specs=[VMEM] * len(outs),
        scratch_shapes=[pltpu.VMEM(dims, dtype) for dims, dtype in scratch],
        compiler_params=PARAMS,
    )(*[array for _, array in ins])


def add(a, b):
    return (a.astype(F32) + b.astype(F32)).astype(BF)


def local(
    geo,
    points,
    result_grad,
    lists_one,
    lists_two,
    rotation,
    gain_one,
    qkv_one,
    out_one,
    gain_two,
    qkv_two,
    out_two,
):
    rows, width = points.shape[1:]
    half = width // 2
    total = 2 * rows
    balls = total // BALL

    def swap(array):
        return lax.ppermute(array, "pts", SWAP)

    def across(array, bits):
        pairs = [(core * geo + i, core * geo + (i ^ bit)) for core, bit in enumerate(bits) for i in range(geo)]
        return lax.ppermute(array, ("pts", "geo"), pairs)

    x = points[0]
    grad = result_grad[0]
    lists = jnp.concatenate([lists_one.reshape(-1), lists_two.reshape(-1)])
    rot = rotation.reshape(rows // BALL, BALL)
    x_other = swap(x)
    lists_other = swap(lists)
    grad_other = swap(grad)
    rot_other = swap(rot)
    gain_one = gain_one.reshape(1, width)
    gain_two = gain_two.reshape(1, width)

    mixed, q, kv, normed = call(
        first_forward,
        "first_forward",
        [("s", lists), ("s", lists_other)] + [("v", a) for a in (x, x_other, gain_one, qkv_one)],
        [shape((total, half)), shape((total, half)), shape((total, width)), shape((total, width))],
    )
    mixed_other = swap(mixed)
    blocks = ((balls, half, BALL), F32)
    moved, mixed_two, part_two, keep_two, send_two = call(
        second_layer,
        "second_layer",
        [("s", lists), ("s", lists_other)]
        + [
            ("v", a)
            for a in (
                rot, rot_other, x, x_other, mixed, mixed_other, grad, grad_other, out_one, gain_two, qkv_two, out_two
            )
        ],
        [shape((total, width)), shape((total, half)), shape((total, width))] + [shape((PIECES // 2, width, half))] * 2,
        [
            ((total, width), BF),
            ((total, width), BF),
            ((total, width), BF),
            ((total, width), BF),
            ((total, half), BF),
            ((total, width), BF),
            ((total, half), BF),
            ((total, half), BF),
            blocks,
            blocks,
            ((PIECES, width, half), BF),
        ],
    )
    part_two_other = swap(part_two)
    core = lax.axis_index("pts")
    mixed_two_other = swap(lax.dynamic_slice_in_dim(mixed_two, (1 - core) * rows, rows, 0))
    keep, send, part_keep, part_send, hidden_grad = call(
        first_backward,
        "first_backward",
        [("s", lists), ("s", lists_other)]
        + [
            ("v", a)
            for a in (
                rot, rot_other, part_two, part_two_other, moved, grad, grad_other, gain_two,
                mixed, normed, q, kv, qkv_one, out_one,
            )
        ],
        [shape((PIECES // 2, width, half))] * 2 + [shape((rows, width))] * 3,
        [
            ((total, width), BF),
            ((total, width), BF),
            ((total, half), BF),
            ((total, half), BF),
            blocks,
            blocks,
            ((PIECES, width, half), BF),
        ],
    )
    part_other = swap(part_send)
    ups = [1 << i for i in range(2, geo.bit_length() - 1)]
    highs = list(zip(ups, ups[1:] + ups[:1]))

    def reduce(keep, send):
        summed = add(keep, across(send, (2, 1)))
        summed = add(summed[:1], across(summed[1:], (1, 2)))
        for bits in highs:
            summed = add(summed, across(summed, bits))
        near = jnp.concatenate([summed, across(summed, (1, 2))], axis=0)
        far = across(near, (2, 1))
        return near, far, swap(near), swap(far)

    pieces_two = reduce(keep_two, send_two)
    pieces_one = reduce(keep, send)
    points_grad, result = call(
        finish_rows,
        "finish_rows",
        [
            ("v", a)
            for a in (part_keep, part_other, x, gain_one, hidden_grad, moved, mixed_two, mixed_two_other, out_two)
        ],
        [shape((rows, width))] * 2,
        [((rows, width), BF)],
    )
    vector, matrix, square = (shape(dims, F32) for dims in ((1, width), (width, 3 * width), (width, width)))
    grads = []
    for pieces, gain, weight in ((pieces_one, gain_one, qkv_one), (pieces_two, gain_two, qkv_two)):
        found = call(
            finish_weights,
            "finish_weights",
            [("v", a) for a in pieces + (gain, weight)],
            [vector, matrix, square],
            [((2, PIECES, width, half), BF)],
        )
        grads += [found[0].reshape(width), found[1], found[2]]
    return (result[None], points_grad[None], *grads)


def solution(mesh):
    rows = P("geo", "pts", None)
    placed = (rows,) * 4 + (P("geo", "pts"),) + (P(),) * 6
    return jax.shard_map(
        functools.partial(local, mesh.shape["geo"]),
        mesh=mesh,
        in_specs=placed,
        out_specs=(rows, rows) + (P(),) * 6,
        check_vma=False,
    )
```

```python
import functools

import jax
import jax.numpy as jnp
from jax import lax
from jax.experimental import pallas as pl
from jax.experimental.pallas import tpu as pltpu
from jax.sharding import PartitionSpec as P

HEADS = 4
BALL = 128
LISTED = 4
EPSILON = 1e-06
BF = jnp.bfloat16
F32 = jnp.float32
SWAP = ((0, 1), (1, 0))

VMEM = pl.BlockSpec(memory_space=pltpu.VMEM)
SMEM = pl.BlockSpec(memory_space=pltpu.SMEM)
HBM = pl.BlockSpec(memory_space=pltpu.HBM)
PARAMS = pltpu.CompilerParams(vmem_limit_bytes=40 * 1024 * 1024)


def dot(a, b, dims=((1,), (0,))):
    return lax.dot_general(a, b, (dims, ((), ())), preferred_element_type=F32)


def norm_factor(x):
    return lax.rsqrt(jnp.mean(x * x, axis=-1, keepdims=True) + EPSILON)


def part_of(place, size):
    return pl.ds(pl.multiple_of(place * size, size), size)


def gain_row(gain):
    return gain[...].astype(F32).reshape(1, gain.shape[0])


def project(normed, columns):
    qkv = dot(normed, columns)
    half = columns.shape[1] // 3
    scale = (2 * half // HEADS) ** (-0.5)
    return qkv[:, :half].astype(BF) * BF(scale), qkv[:, half:].astype(BF)


def stack_heads(rows):
    lane = lax.broadcasted_iota(jnp.int32, rows.shape, 1)
    first = lane < rows.shape[1] // 2
    zero = jnp.zeros_like(rows)
    return jnp.concatenate([jnp.where(first, rows, zero), jnp.where(first, zero, rows)], axis=0)


def unstack_heads(stacked):
    rows = stacked.shape[0] // 2
    lane = lax.broadcasted_iota(jnp.int32, (rows, stacked.shape[1]), 1)
    return jnp.where(lane < stacked.shape[1] // 2, stacked[:rows], stacked[rows:])


def listed_balls(ball, mine, other, core):
    local_balls = mine.shape[1]
    lists, row = (mine, ball) if ball < local_balls else (other, ball - local_balls)
    return [lax.rem(lists[0, row, j] + core * local_balls, 2 * local_balls) for j in range(LISTED)]


def pick(ref, listed, first, half):
    return jnp.concatenate([ref[part_of(i, BALL), first : first + half] for i in listed], axis=0)


def softmax_parts(stacked, keys):
    scores = dot(stacked, keys, ((1,), (1,)))
    exponent = jnp.exp(scores - jnp.max(scores, axis=-1, keepdims=True))
    return exponent, 1.0 / jnp.sum(exponent, axis=-1, keepdims=True)


def mix(exponent, inverse, values):
    return unstack_heads(dot(exponent.astype(BF), values) * inverse)


def ball_backward(stacked, keys, values, exponent, inverse, mixed, mixed_grad):
    grad = stack_heads(mixed_grad.astype(F32)) * inverse
    inner = jnp.sum(grad * jnp.concatenate([mixed, mixed], axis=0), axis=-1, keepdims=True)
    grad = grad.astype(BF)
    scores_grad = (exponent * (dot(grad, values, ((1,), (1,))) - inner)).astype(BF)
    scale = (stacked.shape[1] // 2) ** (-0.5)
    queries_grad = unstack_heads(dot(scores_grad, keys)) * scale
    keys_grad = dot(stacked, scores_grad, ((0,), (0,)))
    values_grad = dot(grad, exponent.astype(BF), ((0,), (0,)))
    return queries_grad.astype(BF), keys_grad, values_grad


def add_listed(ref, listed, part):
    for j, i in enumerate(listed):
        ref[i] += part[:, j * BALL : (j + 1) * BALL]


def key_value_grads(dk_ref, dv_ref):
    balls = dk_ref.shape[0]
    parts = [jnp.concatenate([ref[i].T for i in range(balls)], axis=0).astype(BF) for ref in (dk_ref, dv_ref)]
    return jnp.concatenate(parts, axis=1)


def slot_bit(core):
    geo = lax.axis_index("geo")
    return jnp.where(core == 0, lax.rem(geo // 2, 2), lax.rem(geo, 2))


def weight_part(part, normed_ref, grads, mixed, grad_out_ref):
    half = mixed.shape[1]
    weight = dot(normed_ref[:, part_of(part, half)], grads, ((0,), (0,)))
    out = dot(mixed, grad_out_ref[:, part_of(part, half)], ((0,), (0,)))
    blocks = [weight[:, i * half : (i + 1) * half] for i in range(3)] + [out]
    return jnp.concatenate(blocks, axis=0).astype(BF)


def norm_backward(normed_grad, x, gain, grad_out):
    factor = norm_factor(x)
    scaled = normed_grad.astype(BF).astype(F32) * gain
    inner = jnp.mean(scaled * x, axis=-1, keepdims=True)
    return (grad_out.astype(F32) + factor * scaled - x * (factor * factor * factor) * inner).astype(BF)


def norm_project(x, gain, columns):
    normed = (x * norm_factor(x) * gain).astype(BF)
    return (normed, *project(normed, columns))


def project_mine(
    x_hbm, grad_hbm, rot_hbm, gain_one_hbm, gain_two_hbm, qkv_one_hbm, qkv_two_hbm, out_one_hbm, out_two_hbm,
    x, grad, rot, gain_one, gain_two, qkv_one, qkv_two, out_one, out_two, normed_ref, q_ref, kv_ref,
    sems,
):
    core = lax.axis_index("pts")
    half = x.shape[1] // 2
    copies = []

    def start(source, target):
        copies.append(pltpu.make_async_copy(source, target, sems.at[len(copies)]))
        copies[-1].start()

    def start_columns(source, target):
        for i in range(3):
            start(source.at[:, part_of(2 * i + core, half)], target.at[:, i * half : (i + 1) * half])

    start(x_hbm, x)
    start(gain_one_hbm, gain_one)
    start_columns(qkv_one_hbm, qkv_one)
    first = len(copies)
    start(grad_hbm, grad)
    start(rot_hbm, rot)
    start(gain_two_hbm, gain_two)
    start_columns(qkv_two_hbm, qkv_two)
    for source, target in ((out_one_hbm, out_one), (out_two_hbm, out_two)):
        start(source.at[part_of(core, half)], target.at[:half])
        start(source.at[part_of(1 - core, half)], target.at[half:])
    for copy in copies[:first]:
        copy.wait()
    normed_ref[...], q_ref[...], kv_ref[...] = norm_project(x[...].astype(F32), gain_row(gain_one), qkv_one[...])
    for copy in copies[first:]:
        copy.wait()


def first_forward(
    mine, other, x_other, gain, columns, normed_mine, q_mine, kv_mine, mixed_ref, q_ref, kv_ref, normed_ref
):
    core = lax.axis_index("pts")
    local, width = x_other.shape
    half = width // 2
    normed_ref[:local], q_ref[:local], kv_ref[:local] = normed_mine[...], q_mine[...], kv_mine[...]
    found = norm_project(x_other[...].astype(F32), gain_row(gain), columns[...])
    normed_ref[local:], q_ref[local:], kv_ref[local:] = found
    for ball in range(2 * local // BALL):
        listed = listed_balls(ball, mine, other, core)
        at = slice(ball * BALL, (ball + 1) * BALL)
        stacked = stack_heads(q_ref[at, :])
        exponent, inverse = softmax_parts(stacked, pick(kv_ref, listed, 0, half))
        mixed_ref[at, :] = mix(exponent, inverse, pick(kv_ref, listed, half, half)).astype(BF)


def before_second(
    rot_mine, rot_other, x_mine, x_other, mixed, grad_mine, grad_other, out_one, out_two,
    base_ref, chosen_ref, grad_ref, mg_ref,
):
    core = lax.axis_index("pts")
    local, width = x_mine.shape
    half = width // 2
    total = 2 * local
    own = out_one[:half]
    base_ref[:local] = x_mine[...].astype(F32) + dot(mixed[:local], own)
    base_ref[local:] = x_other[...].astype(F32) + dot(mixed[local:], own)
    grad_ref[:local] = grad_mine[...]
    grad_ref[local:] = grad_other[...]
    mg_ref[...] = dot(grad_ref[...], out_two[:half], ((1,), (1,))).astype(BF)
    lane = lax.broadcasted_iota(jnp.int32, (BALL, total), 1)
    lane = lax.rem(lane + core * local, total).astype(F32)
    for side, ref in enumerate((rot_mine, rot_other)):
        for j in range(local // BALL):
            row = ref[j : j + 1, :].astype(F32)
            column = jnp.broadcast_to(row, (BALL, BALL)).T[:, :1]
            first = side * local + j * BALL
            chosen_ref[first : first + BALL, :] = (lane == column).astype(BF)


def second_layer(
    mine, other, base, mixed_other, chosen, mg_ref, out_one, gain, columns,
    moved_ref, normed_ref, mixed_ref, mixed_send, grads_ref, part_ref,
    hidden_ref, q_ref, kv_ref, dk_ref, dv_ref,
):
    core = lax.axis_index("pts")
    total, width = base.shape
    local = total // 2
    half = width // 2
    far = out_one[half:]
    hidden_ref[:local] = (base[:local] + dot(mixed_other[local:], far)).astype(BF)
    hidden_ref[local:] = (base[local:] + dot(mixed_other[:local], far)).astype(BF)
    moved = dot(chosen[...], hidden_ref[...])
    moved_ref[...] = moved.astype(BF)
    normed_ref[...], q_ref[...], kv_ref[...] = norm_project(moved, gain_row(gain), columns[...])
    dk_ref[...] = jnp.zeros_like(dk_ref)
    dv_ref[...] = jnp.zeros_like(dv_ref)
    for ball in range(total // BALL):
        listed = listed_balls(ball, mine, other, core)
        at = slice(ball * BALL, (ball + 1) * BALL)
        stacked = stack_heads(q_ref[at, :])
        keys = pick(kv_ref, listed, 0, half)
        values = pick(kv_ref, listed, half, half)
        exponent, inverse = softmax_parts(stacked, keys)
        mixed = mix(exponent, inverse, values)
        mixed_ref[at, :] = mixed.astype(BF)
        dq, dk, dv = ball_backward(stacked, keys, values, exponent, inverse, mixed, mg_ref[at, :])
        grads_ref[at, :half] = dq
        add_listed(dk_ref, listed, dk)
        add_listed(dv_ref, listed, dv)
    grads_ref[:, half:] = key_value_grads(dk_ref, dv_ref)
    part_ref[...] = dot(grads_ref[...], columns[...], ((1,), (1,))).astype(BF)
    mixed_send[...] = mixed_ref[local:]


def second_weights(normed, grads, mixed, grad, keep_ref, send_ref):
    bit = slot_bit(lax.axis_index("pts"))
    send_ref[...] = weight_part(1 - bit, normed, grads[...], mixed[...], grad)
    keep_ref[...] = weight_part(bit, normed, grads[...], mixed[...], grad)


def first_backward(
    mine, other, rot_mine, rot_other, part_mine, part_other, moved, grad, gain_two,
    mixed_ref, normed, q_ref, kv_ref, out_one,
    hg_ref, grads_ref, send_ref,
    rows_grad_ref, mg_ref, dk_ref, dv_ref,
):
    core = lax.axis_index("pts")
    total, width = grad.shape
    local = total // 2
    half = width // 2
    gain = gain_row(gain_two)
    for first, far in ((0, local), (local, 0)):
        at = slice(first, first + local)
        normed_grad = part_mine[at].astype(F32) + part_other[far : far + local].astype(F32)
        rows_grad_ref[at] = norm_backward(normed_grad, moved[at].astype(F32), gain, grad[at])
    row_of = [ref[j : j + 1, :] for ref in (rot_mine, rot_other) for j in range(local // BALL)]
    order = jnp.concatenate(row_of, axis=1).astype(F32)
    rows_grad = rows_grad_ref[...]
    place = lax.broadcasted_iota(jnp.int32, (BALL, total), 0)
    for j in range(total // BALL):
        first = lax.rem(j * BALL + core * local, total)
        chosen = ((place + first).astype(F32) == order).astype(BF)
        hg_ref[j * BALL : (j + 1) * BALL, :] = dot(chosen, rows_grad).astype(BF)
    mg_ref[...] = dot(hg_ref[...], out_one[:half], ((1,), (1,))).astype(BF)
    dk_ref[...] = jnp.zeros_like(dk_ref)
    dv_ref[...] = jnp.zeros_like(dv_ref)
    for ball in range(total // BALL):
        listed = listed_balls(ball, mine, other, core)
        at = slice(ball * BALL, (ball + 1) * BALL)
        stacked = stack_heads(q_ref[at, :])
        keys = pick(kv_ref, listed, 0, half)
        values = pick(kv_ref, listed, half, half)
        exponent, inverse = softmax_parts(stacked, keys)
        mixed = mixed_ref[at, :].astype(F32)
        dq, dk, dv = ball_backward(stacked, keys, values, exponent, inverse, mixed, mg_ref[at, :])
        grads_ref[at, :half] = dq
        add_listed(dk_ref, listed, dk)
        add_listed(dv_ref, listed, dv)
    grads_ref[:, half:] = key_value_grads(dk_ref, dv_ref)
    send_ref[...] = weight_part(1 - slot_bit(core), normed, grads_ref[...], mixed_ref[...], hg_ref)


def first_weights(normed, grads, mixed, hidden_grad, columns, keep_ref, part_keep, part_send):
    core = lax.axis_index("pts")
    local = part_keep.shape[0]
    part_send[...] = dot(grads[local:], columns[...], ((1,), (1,))).astype(BF)
    part_keep[...] = dot(grads[:local], columns[...], ((1,), (1,)))
    keep_ref[...] = weight_part(slot_bit(core), normed, grads[...], mixed[...], hidden_grad)


def finish_rows(
    part_mine, part_other, x_mine, gain, hidden_grad, moved, mixed, mixed_other, out_two, points_grad, result
):
    local = x_mine.shape[0]
    normed_grad = part_mine[...] + part_other[...].astype(F32)
    points_grad[...] = norm_backward(
        normed_grad, x_mine[...].astype(F32), gain_row(gain), hidden_grad[:local]
    )
    both = jnp.concatenate([mixed[:local], mixed_other[...]], axis=1)
    result[...] = (moved[:local].astype(F32) + dot(both, out_two[...])).astype(BF)


def finish_weights(
    near_mine, far_mine, near_other, far_other, gain, weight, gain_grad, qkv_grad, out_grad, folded_ref
):
    core = lax.axis_index("pts")
    half = near_mine.shape[-1]
    for side, near, far in ((core, near_mine, far_mine), (1 - core, near_other, far_other)):
        bit = slot_bit(side)
        for part, ref in ((bit, near), (1 - bit, far)):
            at = part_of(part, half)
            folded = jnp.zeros((half, half), F32)
            for p in range(3):
                piece = ref[p * half : (p + 1) * half].astype(F32)
                columns = part_of(2 * p + side, half)
                qkv_grad[at, columns] = piece
                folded = folded + piece * weight[at, columns].astype(F32)
            folded_ref[side, at] = folded
            out_grad[part_of(side, half), at] = ref[3 * half :].astype(F32)
    folded = folded_ref[0] + folded_ref[1]
    gain_grad[...] = jnp.sum(folded.T, axis=0, keepdims=True) / gain_row(gain)


def shape(*dims, dtype=BF):
    return jax.ShapeDtypeStruct(dims, dtype)


def call(body, ins, outs, scratch=(), lists=()):
    return pl.pallas_call(
        body,
        name=body.__name__,
        out_shape=outs,
        in_specs=[SMEM] * len(lists) + [VMEM] * len(ins),
        out_specs=[VMEM] * len(outs),
        scratch_shapes=[pltpu.VMEM(item.shape, item.dtype) for item in scratch],
        compiler_params=PARAMS,
    )(*lists, *ins)


def add(a, b):
    return (a.astype(F32) + b.astype(F32)).astype(BF)


def local(
    geo,
    points,
    result_grad,
    lists_one,
    lists_two,
    rotation,
    gain_one,
    qkv_one,
    out_one,
    gain_two,
    qkv_two,
    out_two,
):
    rows, width = points.shape[1:]
    half = width // 2
    total = 2 * rows
    balls = total // BALL
    thin, wide, triple = shape(total, half), shape(total, width), shape(total, 3 * half)
    blocks = shape(balls, half, BALL, dtype=F32)
    weights = shape(4 * half, half)

    def swap(array):
        return lax.ppermute(array, "pts", SWAP)

    def across(array, bits):
        pairs = [(core * geo + i, core * geo + (i ^ bit)) for core, bit in enumerate(bits) for i in range(geo)]
        return lax.ppermute(array, ("pts", "geo"), pairs)

    ups = [1 << i for i in range(2, geo.bit_length() - 1)]
    doublings = [(1, 2)] + list(zip(ups, ups[1:] + ups[:1]))

    def reduce(summed):
        for bits in doublings:
            summed = add(summed, across(summed, bits))
        far = across(summed, (2, 1))
        return [summed, far, swap(summed), swap(far)]

    x = points[0]
    grad = result_grad[0]
    rot = rotation.reshape(rows // BALL, BALL)
    x_other = swap(x)
    one = [lists_one, swap(lists_one)]
    grad_other = swap(grad)
    rot_other = swap(rot)
    two = [lists_two, swap(lists_two)]
    arguments = (x, grad, rot, gain_one, gain_two, qkv_one, qkv_two, out_one, out_two)
    own_rows = shape(rows, width)
    own_columns = shape(width, 3 * half)
    square = shape(width, width)
    x, grad, rot, near_gain, far_gain, columns_one, columns_two, out_one, out_two, *projected = pl.pallas_call(
        project_mine,
        name="project_mine",
        out_shape=[own_rows, own_rows, shape(*rot.shape, dtype=rot.dtype), gain_one, gain_two]
        + [own_columns, own_columns, square, square, own_rows, shape(rows, half), own_rows],
        in_specs=[HBM] * 9,
        out_specs=[VMEM] * 12,
        scratch_shapes=[pltpu.SemaphoreType.DMA((15,))],
        compiler_params=PARAMS,
    )(*[pltpu.with_memory_space_constraint(a, pltpu.HBM) for a in arguments])
    mixed, q, kv, normed = call(
        first_forward, [x_other, near_gain, columns_one, *projected], [thin, thin, wide, wide], lists=one
    )
    mixed_other = swap(mixed)
    base, chosen, grads_in, mg = call(
        before_second,
        [rot, rot_other, x, x_other, mixed, grad, grad_other, out_one, out_two],
        [shape(total, width, dtype=F32), shape(total, total), wide, thin],
    )
    moved, normed_two, mixed_two, mixed_send, grads_two, part_two = call(
        second_layer,
        [base, mixed_other, chosen, mg, out_one, far_gain, columns_two],
        [wide, wide, thin, shape(rows, half), triple, wide],
        [wide, thin, wide, blocks, blocks],
        two,
    )
    part_two_other = swap(part_two)
    mixed_two_other = swap(mixed_send)
    keep_two, send_two = call(second_weights, [normed_two, grads_two, mixed_two, grads_in], [weights, weights])
    summed_two = add(keep_two, across(send_two, (2, 1)))
    hidden_grad, grads_one, send = call(
        first_backward,
        [rot, rot_other, part_two, part_two_other, moved, grads_in, far_gain, mixed, normed, q, kv, out_one],
        [wide, triple, weights],
        [wide, thin, blocks, blocks],
        one,
    )
    received = across(send, (2, 1))
    keep, part_keep, part_send = call(
        first_weights,
        [normed, grads_one, mixed, hidden_grad, columns_one],
        [weights, shape(rows, width, dtype=F32), shape(rows, width)],
    )
    points_grad, result = call(
        finish_rows,
        [part_keep, swap(part_send), x, near_gain, hidden_grad, moved, mixed_two, mixed_two_other, out_two],
        [shape(rows, width)] * 2,
    )
    summed = add(keep, received)
    summed, points_grad, result = lax.optimization_barrier((summed, points_grad, result))
    pieces_two = reduce(summed_two)
    pieces_one = reduce(summed)
    grads = []
    for pieces, gain, weight in ((pieces_one, near_gain, qkv_one), (pieces_two, far_gain, qkv_two)):
        found = call(
            finish_weights,
            pieces + [gain, weight],
            [shape(*dims, dtype=F32) for dims in ((1, width), (width, 3 * width), (width, width))],
            [shape(2, width, half, dtype=F32)],
        )
        grads += [found[0].reshape(width), found[1], found[2]]
    return (result[None], points_grad[None], *grads)


def solution(mesh):
    rows = P("geo", "pts", None)
    placed = (rows,) * 4 + (P("geo", "pts"),) + (P(),) * 6
    return jax.shard_map(
        functools.partial(local, mesh.shape["geo"]),
        mesh=mesh,
        in_specs=placed,
        out_specs=(rows, rows) + (P(),) * 6,
        check_vma=False,
    )
```

```python
import functools

import jax
import jax.numpy as jnp
from jax import lax
from jax.experimental import pallas as pl
from jax.experimental.pallas import tpu as pltpu
from jax.sharding import PartitionSpec as P

HEADS = 4
BALL = 128
LISTED = 4
CHUNK = 256
QUARTERED = (True, True)
EPSILON = 1e-06
BF = jnp.bfloat16
F32 = jnp.float32
SWAP = ((0, 1), (1, 0))

VMEM = pl.BlockSpec(memory_space=pltpu.VMEM)
SMEM = pl.BlockSpec(memory_space=pltpu.SMEM)
HBM = pl.BlockSpec(memory_space=pltpu.HBM)
PARAMS = pltpu.CompilerParams(vmem_limit_bytes=40 * 1024 * 1024)


def dot(a, b, dims=((1,), (0,))):
    return lax.dot_general(a, b, (dims, ((), ())), preferred_element_type=F32)


def norm_factor(x):
    return lax.rsqrt(jnp.mean(x * x, axis=-1, keepdims=True) + EPSILON)


def part_of(place, size):
    return pl.ds(pl.multiple_of(place * size, size), size)


def gain_row(gain):
    return gain[...].astype(F32).reshape(1, gain.shape[0])


def project(normed, columns):
    qkv = dot(normed, columns)
    half = columns.shape[1] // 3
    scale = (2 * half // HEADS) ** (-0.5)
    return qkv[:, :half].astype(BF) * BF(scale), qkv[:, half:].astype(BF)


def stack_heads(rows):
    lane = lax.broadcasted_iota(jnp.int32, rows.shape, 1)
    first = lane < rows.shape[1] // 2
    zero = jnp.zeros_like(rows)
    return jnp.concatenate([jnp.where(first, rows, zero), jnp.where(first, zero, rows)], axis=0)


def unstack_heads(stacked):
    rows = stacked.shape[0] // 2
    lane = lax.broadcasted_iota(jnp.int32, (rows, stacked.shape[1]), 1)
    return jnp.where(lane < stacked.shape[1] // 2, stacked[:rows], stacked[rows:])


def listed_balls(ball, mine, other, core):
    local_balls = mine.shape[1]
    lists, row = (mine, ball) if ball < local_balls else (other, ball - local_balls)
    return [lax.rem(lists[0, row, j] + core * local_balls, 2 * local_balls) for j in range(LISTED)]


def pick(ref, listed, first, half):
    return jnp.concatenate([ref[part_of(i, BALL), first : first + half] for i in listed], axis=0)


def in_stages(count, *stages):
    held = {}
    for step in range(count + len(stages) - 1):
        for depth, stage in enumerate(stages):
            ball = step - depth
            if 0 <= ball < count:
                held[ball] = stage(ball, *held.pop(ball, ()))


def softmax_parts(scores):
    exponent = jnp.exp(scores - jnp.max(scores, axis=-1, keepdims=True))
    return exponent, 1.0 / jnp.sum(exponent, axis=-1, keepdims=True)


def backward_stages(lists, core, q_ref, kv_ref, mg_ref, mixed_ref, grads_ref, dk_ref, dv_ref, forward):
    half = q_ref.shape[1]
    scale = (half // 2) ** (-0.5)

    def products(ball):
        at = slice(ball * BALL, (ball + 1) * BALL)
        listed = listed_balls(ball, *lists, core)
        stacked, grad = stack_heads(q_ref[at, :]), stack_heads(mg_ref[at, :])
        scores = dot(stacked, pick(kv_ref, listed, 0, half), ((1,), (1,)))
        weights_grad = dot(grad, pick(kv_ref, listed, half, half), ((1,), (1,)))
        return listed, stacked, grad, scores, weights_grad

    def elements(ball, listed, stacked, grad, scores, weights_grad):
        exponent, inverse = softmax_parts(scores)
        attention = exponent * inverse
        if forward:
            inner = jnp.sum(attention * weights_grad, axis=-1, keepdims=True)
        else:
            mixed = mixed_ref[ball * BALL : (ball + 1) * BALL, :].astype(F32)
            inner = jnp.sum(grad.astype(F32) * jnp.concatenate([mixed, mixed], axis=0), axis=-1, keepdims=True)
        scores_grad = attention * (weights_grad - inner)
        return listed, stacked, grad, attention.astype(BF), scores_grad.astype(BF)

    def gradients(ball, listed, stacked, grad, attention, scores_grad):
        at = slice(ball * BALL, (ball + 1) * BALL)
        if forward:
            mixed_ref[at, :] = unstack_heads(dot(attention, pick(kv_ref, listed, half, half))).astype(BF)
        queries_grad = unstack_heads(dot(scores_grad, pick(kv_ref, listed, 0, half))) * scale
        grads_ref[at, :half] = queries_grad.astype(BF)
        add_listed(dk_ref, listed, dot(stacked, scores_grad, ((0,), (0,))))
        add_listed(dv_ref, listed, dot(grad, attention, ((0,), (0,))))
        return ()

    dk_ref[...] = jnp.zeros_like(dk_ref)
    dv_ref[...] = jnp.zeros_like(dv_ref)
    in_stages(q_ref.shape[0] // BALL, products, elements, gradients)


def add_listed(ref, listed, part):
    for j, i in enumerate(listed):
        ref[i] += part[:, j * BALL : (j + 1) * BALL]


def normed_grads(grads_ref, dk_ref, dv_ref, columns, store):
    half = dk_ref.shape[1]

    def turn(ball):
        at = slice(ball * BALL, (ball + 1) * BALL)
        grads_ref[at, half : 2 * half] = dk_ref[ball].T.astype(BF)
        grads_ref[at, 2 * half :] = dv_ref[ball].T.astype(BF)
        return ()

    def multiply(ball):
        at = slice(ball * BALL, (ball + 1) * BALL)
        store(at, dot(grads_ref[at, :], columns, ((1,), (1,))))
        return ()

    in_stages(dk_ref.shape[0], turn, multiply)


def geo_bit(bit):
    return lax.rem(lax.axis_index("geo") // bit, 2)


def kept(core, quartered):
    half = geo_bit(jnp.where(core == 0, 2, 1))
    return half, geo_bit(jnp.where(core == 0, 1, 2)) if quartered else 0


def store_quarters(ref, blocks, slot):
    size = ref.shape[1]
    ref[slot] = blocks[:size]
    ref[1 - slot] = blocks[size:]


def weight_part(part, normed_ref, grads, mixed, grad_out_ref):
    half = mixed.shape[1]
    weight = dot(normed_ref[:, part_of(part, half)], grads, ((0,), (0,)))
    out = dot(mixed, grad_out_ref[:, part_of(part, half)], ((0,), (0,)))
    blocks = [weight[:, i * half : (i + 1) * half] for i in range(3)] + [out]
    return jnp.concatenate(blocks, axis=0).astype(BF)


def norm_backward(normed_grad, x, gain, grad_out):
    factor = norm_factor(x)
    scaled = normed_grad.astype(BF).astype(F32) * gain
    inner = jnp.mean(scaled * x, axis=-1, keepdims=True)
    return (grad_out.astype(F32) + factor * scaled - x * (factor * factor * factor) * inner).astype(BF)


def norm_project(rows_count, rows_of, gain, columns, normed_ref, q_ref, kv_ref, first=0):
    def norm(chunk, x):
        return ((x * norm_factor(x) * gain).astype(BF),)

    def store(chunk, normed):
        at = slice(first + chunk * CHUNK, first + (chunk + 1) * CHUNK)
        normed_ref[at], (q_ref[at], kv_ref[at]) = normed, project(normed, columns)
        return ()

    in_stages(rows_count // CHUNK, lambda chunk: (rows_of(slice(chunk * CHUNK, (chunk + 1) * CHUNK)),), norm, store)


def project_mine(
    x_hbm, grad_hbm, rot_hbm, lists_one_hbm, lists_two_hbm, gain_one_hbm, gain_two_hbm, qkv_one_hbm, qkv_two_hbm, out_one_hbm, out_two_hbm,
    x, grad, rot, lists_one, lists_two, gain_one, gain_two, qkv_one, qkv_two, out_one, out_two,
    normed_ref, q_ref, kv_ref, sems,
):
    core = lax.axis_index("pts")
    half = x.shape[1] // 2
    copies = []

    def start(source, target):
        copies.append(pltpu.make_async_copy(source, target, sems.at[len(copies)]))
        copies[-1].start()

    def start_columns(source, target):
        for i in range(3):
            start(source.at[:, part_of(2 * i + core, half)], target.at[:, i * half : (i + 1) * half])

    start(x_hbm, x)
    start(gain_one_hbm, gain_one)
    start_columns(qkv_one_hbm, qkv_one)
    first = len(copies)
    start(grad_hbm, grad)
    start(rot_hbm, rot)
    start(lists_one_hbm, lists_one)
    start(lists_two_hbm, lists_two)
    start(gain_two_hbm, gain_two)
    start_columns(qkv_two_hbm, qkv_two)
    for source, target in ((out_one_hbm, out_one), (out_two_hbm, out_two)):
        start(source.at[part_of(core, half)], target.at[:half])
        start(source.at[part_of(1 - core, half)], target.at[half:])
    for copy in copies[:first]:
        copy.wait()
    norm_project(
        x.shape[0], lambda at: x[at].astype(F32), gain_row(gain_one), qkv_one[...], normed_ref, q_ref, kv_ref
    )
    for copy in copies[first:]:
        copy.wait()


def first_forward(
    mine, other, x_other, gain, columns, normed_mine, q_mine, kv_mine, mixed_ref, q_ref, kv_ref, normed_ref
):
    core = lax.axis_index("pts")
    local, width = x_other.shape
    half = width // 2
    normed_ref[:local], q_ref[:local], kv_ref[:local] = normed_mine[...], q_mine[...], kv_mine[...]
    norm_project(
        local, lambda at: x_other[at].astype(F32), gain_row(gain), columns[...], normed_ref, q_ref, kv_ref, local
    )

    def products(ball):
        listed = listed_balls(ball, mine, other, core)
        stacked = stack_heads(q_ref[ball * BALL : (ball + 1) * BALL, :])
        return listed, dot(stacked, pick(kv_ref, listed, 0, half), ((1,), (1,)))

    def elements(ball, listed, scores):
        exponent, inverse = softmax_parts(scores)
        return listed, exponent.astype(BF), inverse

    def outputs(ball, listed, exponent, inverse):
        mixed = unstack_heads(dot(exponent, pick(kv_ref, listed, half, half)) * inverse)
        mixed_ref[ball * BALL : (ball + 1) * BALL, :] = mixed.astype(BF)
        return ()

    in_stages(2 * local // BALL, products, elements, outputs)


def before_second(
    rot_mine, rot_other, x_mine, x_other, mixed, grad_mine, grad_other, out_one, out_two,
    base_ref, chosen_ref, chosen_back, grad_ref, mg_ref,
):
    core = lax.axis_index("pts")
    local, width = x_mine.shape
    half = width // 2
    total = 2 * local
    own = out_one[:half]
    base_ref[:local] = x_mine[...].astype(F32) + dot(mixed[:local], own)
    base_ref[local:] = x_other[...].astype(F32) + dot(mixed[local:], own)
    grad_ref[:local] = grad_mine[...]
    grad_ref[local:] = grad_other[...]
    mg_ref[...] = dot(grad_ref[...], out_two[:half], ((1,), (1,))).astype(BF)
    lane = lax.broadcasted_iota(jnp.int32, (BALL, total), 1)
    lane = lax.rem(lane + core * local, total).astype(F32)
    for side, ref in enumerate((rot_mine, rot_other)):
        for j in range(local // BALL):
            row = ref[j : j + 1, :].astype(F32)
            column = jnp.broadcast_to(row, (BALL, BALL)).T[:, :1]
            first = side * local + j * BALL
            chosen_ref[first : first + BALL, :] = (lane == column).astype(BF)
    row_of = [ref[j : j + 1, :] for ref in (rot_mine, rot_other) for j in range(local // BALL)]
    order = lax.rem(jnp.concatenate(row_of, axis=1) + core * local, total)
    place = lax.broadcasted_iota(jnp.int32, (BALL, total), 0)
    for first in range(0, total, BALL):
        chosen_back[first : first + BALL, :] = (place == order - first).astype(BF)


def second_layer(
    mine, other, base, mixed_other, chosen, mg_ref, out_one, gain, columns,
    moved_ref, normed_ref, mixed_ref, mixed_send, grads_ref, part_ref,
    hidden_ref, q_ref, kv_ref, dk_ref, dv_ref,
):
    core = lax.axis_index("pts")
    total, width = base.shape
    local = total // 2
    half = width // 2
    far = out_one[half:]
    for first in range(0, total, CHUNK):
        other_first = (first + local) % total
        added = dot(mixed_other[other_first : other_first + CHUNK], far)
        hidden_ref[first : first + CHUNK] = (base[first : first + CHUNK] + added).astype(BF)

    def rotate(at):
        moved = dot(chosen[at], hidden_ref[...])
        moved_ref[at] = moved.astype(BF)
        return moved

    norm_project(total, rotate, gain_row(gain), columns[...], normed_ref, q_ref, kv_ref)
    backward_stages((mine, other), core, q_ref, kv_ref, mg_ref, mixed_ref, grads_ref, dk_ref, dv_ref, True)

    def store(at, part):
        part_ref[at] = part.astype(BF)

    normed_grads(grads_ref, dk_ref, dv_ref, columns[...], store)
    mixed_send[...] = mixed_ref[local:]


def second_weights(normed, grads, mixed, grad, keep_ref, send_ref):
    part, slot = kept(lax.axis_index("pts"), QUARTERED[1])
    store_quarters(send_ref, weight_part(1 - part, normed, grads[...], mixed[...], grad), slot)
    store_quarters(keep_ref, weight_part(part, normed, grads[...], mixed[...], grad), slot)


def first_backward(
    mine, other, chosen_back, part_mine, part_other, moved, grad, gain_two,
    mixed_ref, normed, q_ref, kv_ref, out_one, columns,
    hg_ref, grads_ref, send_ref, part_keep, part_send,
    rows_grad_ref, mg_ref, dk_ref, dv_ref,
):
    core = lax.axis_index("pts")
    total, width = grad.shape
    local = total // 2
    half = width // 2
    gain = gain_row(gain_two)
    for first, far in ((0, local), (local, 0)):
        at = slice(first, first + local)
        normed_grad = part_mine[at].astype(F32) + part_other[far : far + local].astype(F32)
        rows_grad_ref[at] = norm_backward(normed_grad, moved[at].astype(F32), gain, grad[at])

    def rotate(chunk):
        return (dot(chosen_back[chunk * CHUNK : (chunk + 1) * CHUNK], rows_grad_ref[...]).astype(BF),)

    def project_back(chunk, hidden_grad):
        at = slice(chunk * CHUNK, (chunk + 1) * CHUNK)
        hg_ref[at] = hidden_grad
        mg_ref[at] = dot(hidden_grad, out_one[:half], ((1,), (1,))).astype(BF)
        return ()

    in_stages(total // CHUNK, rotate, project_back)
    backward_stages((mine, other), core, q_ref, kv_ref, mg_ref, mixed_ref, grads_ref, dk_ref, dv_ref, False)

    def store(at, part):
        if at.start < local:
            part_keep[at] = part
        else:
            part_send[at.start - local : at.stop - local] = part.astype(BF)

    normed_grads(grads_ref, dk_ref, dv_ref, columns[...], store)
    part, slot = kept(core, QUARTERED[0])
    store_quarters(send_ref, weight_part(1 - part, normed, grads_ref[...], mixed_ref[...], hg_ref), slot)


def finish_rows(
    normed, grads, mixed, hidden_grad, part_mine, part_other, x_mine, gain, moved, mixed_two, mixed_two_other, out_two,
    keep_ref, points_grad, result,
):
    local = x_mine.shape[0]
    part, slot = kept(lax.axis_index("pts"), QUARTERED[0])
    store_quarters(keep_ref, weight_part(part, normed, grads[...], mixed[...], hidden_grad), slot)
    normed_grad = part_mine[...] + part_other[...].astype(F32)
    points_grad[...] = norm_backward(
        normed_grad, x_mine[...].astype(F32), gain_row(gain), hidden_grad[:local]
    )
    both = jnp.concatenate([mixed_two[:local], mixed_two_other[...]], axis=1)
    result[...] = (moved[:local].astype(F32) + dot(both, out_two[...])).astype(BF)


def finish_weights(
    quartered, near_mine, far_mine, near_other, far_other, gain, weight, gain_grad, qkv_grad, out_grad, folded_ref
):
    core = lax.axis_index("pts")
    size, half = near_mine.shape[1:]
    for side, near, far in ((core, near_mine, far_mine), (1 - core, near_other, far_other)):
        bit, slot = kept(side, quartered)
        for part, ref in ((bit, near), (1 - bit, far)):

            def block(p):
                first = p * half
                quarter = slot if first < size else 1 - slot
                return ref[quarter, first % size : first % size + half].astype(F32)

            at = part_of(part, half)
            folded = jnp.zeros((half, half), F32)
            for p in range(3):
                columns = part_of(2 * p + side, half)
                qkv_grad[at, columns] = block(p)
                folded = folded + block(p) * weight[at, columns].astype(F32)
            folded_ref[side, at] = folded
            out_grad[part_of(side, half), at] = block(3)
    folded = folded_ref[0] + folded_ref[1]
    gain_grad[...] = jnp.sum(folded.T, axis=0, keepdims=True) / gain_row(gain)


def shape(*dims, dtype=BF):
    return jax.ShapeDtypeStruct(dims, dtype)


def call(body, ins, outs, scratch=(), lists=()):
    return pl.pallas_call(
        body,
        name=getattr(body, "func", body).__name__,
        out_shape=outs,
        in_specs=[SMEM] * len(lists) + [VMEM] * len(ins),
        out_specs=[VMEM] * len(outs),
        scratch_shapes=[pltpu.VMEM(item.shape, item.dtype) for item in scratch],
        compiler_params=PARAMS,
    )(*lists, *ins)


def add(a, b):
    return (a.astype(F32) + b.astype(F32)).astype(BF)


def local(
    geo,
    points,
    result_grad,
    lists_one,
    lists_two,
    rotation,
    gain_one,
    qkv_one,
    out_one,
    gain_two,
    qkv_two,
    out_two,
):
    rows, width = points.shape[1:]
    half = width // 2
    total = 2 * rows
    balls = total // BALL
    thin, wide, triple = shape(total, half), shape(total, width), shape(total, 3 * half)
    blocks = shape(balls, half, BALL, dtype=F32)
    weights = shape(2, width, half)

    def swap(array):
        return lax.ppermute(array, "pts", SWAP)

    def across(array, bits):
        pairs = [(core * geo + i, core * geo + (i ^ bit)) for core, bit in enumerate(bits) for i in range(geo)]
        return lax.ppermute(array, ("pts", "geo"), pairs)

    ups = [1 << i for i in range(2, geo.bit_length() - 1)]
    doublings = [(1, 2)] + list(zip(ups, ups[1:] + ups[:1]))

    x = points[0]
    grad = result_grad[0]
    rot = rotation.reshape(rows // BALL, BALL)
    others = [swap(a) for a in (x, lists_one, lists_two, rot, grad)]
    arguments = (x, grad, rot, lists_one, lists_two, gain_one, gain_two, qkv_one, qkv_two, out_one, out_two)
    own_rows = shape(rows, width)
    own_columns = shape(width, 3 * half)
    square = shape(width, width)
    x, grad, rot, *mine, near_gain, far_gain, columns_one, columns_two, out_one, out_two, normed, q, kv = pl.pallas_call(
        project_mine,
        name="project_mine",
        out_shape=[shape(*a.shape, dtype=a.dtype) for a in arguments[:7]]
        + [own_columns, own_columns, square, square, own_rows, shape(rows, half), own_rows],
        in_specs=[HBM] * len(arguments),
        out_specs=[VMEM] * 14,
        scratch_shapes=[pltpu.SemaphoreType.DMA((17,))],
        compiler_params=PARAMS,
    )(*[pltpu.with_memory_space_constraint(a, pltpu.HBM) for a in arguments])
    x_other, one_other, two_other, rot_other, grad_other = lax.optimization_barrier(others)
    one = [mine[0], one_other]
    two = [mine[1], two_other]
    mixed, q, kv, normed = call(
        first_forward, [x_other, near_gain, columns_one, normed, q, kv], [thin, thin, wide, wide], lists=one
    )
    mixed_other = swap(mixed)
    base, chosen, chosen_back, grads_in, mg = call(
        before_second,
        [rot, rot_other, x, x_other, mixed, grad, grad_other, out_one, out_two],
        [shape(total, width, dtype=F32), shape(total, total), shape(total, total), wide, thin],
    )
    moved, normed_two, mixed_two, mixed_send, grads_two, part_two = call(
        second_layer,
        [base, mixed_other, chosen, mg, out_one, far_gain, columns_two],
        [wide, wide, thin, shape(rows, half), triple, wide],
        [wide, thin, wide, blocks, blocks],
        two,
    )
    part_two_other = swap(part_two)
    mixed_two_other = swap(mixed_send)
    keep_two, send_two = call(second_weights, [normed_two, grads_two, mixed_two, grads_in], [weights, weights])
    summed_two = add(keep_two, across(send_two, (2, 1)))
    hidden_grad, grads_one, send, part_keep, part_send = call(
        first_backward,
        [chosen_back, part_two, part_two_other, moved, grads_in, far_gain, mixed, normed, q, kv, out_one, columns_one],
        [wide, triple, weights, shape(rows, width, dtype=F32), own_rows],
        [wide, thin, blocks, blocks],
        one,
    )
    part_other = swap(part_send)
    received = across(send, (2, 1))
    keep, points_grad, result = call(
        finish_rows,
        [normed, grads_one, mixed, hidden_grad, part_keep, part_other, x, near_gain]
        + [moved, mixed_two, mixed_two_other, out_two],
        [weights, own_rows, own_rows],
    )
    summed = add(keep, received)

    first, rest = doublings[0], doublings[1:]

    def second_step(array, quartered):
        return add(array[:1], across(array[1:], first)) if quartered else add(array, across(array, first))

    summed_two = second_step(summed_two, QUARTERED[1])
    summed = second_step(summed, QUARTERED[0])
    for bits in rest:
        summed_two = add(summed_two, across(summed_two, bits))
        summed = add(summed, across(summed, bits))

    def widen(array, quartered):
        return jnp.concatenate([array, across(array, first)], axis=0) if quartered else array

    summed_two = widen(summed_two, QUARTERED[1])
    summed = widen(summed, QUARTERED[0])
    far_two = across(summed_two, (2, 1))
    far = across(summed, (2, 1))
    tied_two, tied_far_two, _ = lax.optimization_barrier((summed_two, far_two, summed))
    pieces_two = [summed_two, far_two, swap(tied_two), swap(tied_far_two)]
    pieces_one = [summed, far, swap(summed), swap(far)]
    grads = []
    for quartered, pieces, gain, weight in (
        (QUARTERED[0], pieces_one, near_gain, qkv_one),
        (QUARTERED[1], pieces_two, far_gain, qkv_two),
    ):
        found = call(
            functools.partial(finish_weights, quartered),
            pieces + [gain, weight],
            [shape(*dims, dtype=F32) for dims in ((1, width), (width, 3 * width), (width, width))],
            [shape(2, width, half, dtype=F32)],
        )
        grads += [found[0].reshape(width), found[1], found[2]]
    return (result[None], points_grad[None], *grads)


def solution(mesh):
    rows = P("geo", "pts", None)
    placed = (rows,) * 4 + (P("geo", "pts"),) + (P(),) * 6
    return jax.shard_map(
        functools.partial(local, mesh.shape["geo"]),
        mesh=mesh,
        in_specs=placed,
        out_specs=(rows, rows) + (P(),) * 6,
        check_vma=False,
    )
```

```python
import functools

import jax
import jax.numpy as jnp
from jax import lax
from jax.experimental import pallas as pl
from jax.experimental.pallas import tpu as pltpu
from jax.sharding import PartitionSpec as P

HEADS = 4
BALL = 128
LISTED = 4
CHUNK = 512
QUARTERED = (True, True)
EPSILON = 1e-06
BF = jnp.bfloat16
F32 = jnp.float32
SWAP = ((0, 1), (1, 0))

VMEM = pl.BlockSpec(memory_space=pltpu.VMEM)
SMEM = pl.BlockSpec(memory_space=pltpu.SMEM)
HBM = pl.BlockSpec(memory_space=pltpu.HBM)
PARAMS = pltpu.CompilerParams(vmem_limit_bytes=40 * 1024 * 1024)


def dot(a, b, dims=((1,), (0,))):
    return lax.dot_general(a, b, (dims, ((), ())), preferred_element_type=F32)


def norm_factor(x):
    return lax.rsqrt(jnp.mean(x * x, axis=-1, keepdims=True) + EPSILON)


def parity(index):
    for shift in (8, 4, 2, 1):
        index = index ^ (index >> shift)
    return index & 1


def own_side():
    return lax.axis_index("pts") ^ parity(lax.axis_index("geo"))


def part_of(place, size):
    return pl.ds(pl.multiple_of(place * size, size), size)


def gain_row(gain):
    return gain[...].astype(F32).reshape(1, gain.shape[0])


def project(normed, columns):
    qkv = dot(normed, columns)
    half = columns.shape[1] // 3
    scale = (2 * half // HEADS) ** (-0.5)
    return qkv[:, :half].astype(BF) * BF(scale), qkv[:, half:].astype(BF)


def stack_heads(rows):
    lane = lax.broadcasted_iota(jnp.int32, rows.shape, 1)
    first = lane < rows.shape[1] // 2
    zero = jnp.zeros_like(rows)
    return jnp.concatenate([jnp.where(first, rows, zero), jnp.where(first, zero, rows)], axis=0)


def unstack_heads(stacked):
    rows = stacked.shape[0] // 2
    lane = lax.broadcasted_iota(jnp.int32, (rows, stacked.shape[1]), 1)
    return jnp.where(lane < stacked.shape[1] // 2, stacked[:rows], stacked[rows:])


def listed_balls(ball, mine, other, core):
    local_balls = mine.shape[1]
    lists, row = (mine, ball) if ball < local_balls else (other, ball - local_balls)
    return [lax.rem(lists[0, row, j] + core * local_balls, 2 * local_balls) for j in range(LISTED)]


def pick(ref, listed, first, half):
    return jnp.concatenate([ref[part_of(i, BALL), first : first + half] for i in listed], axis=0)


def turn_balls(turned_ref, kv_ref):
    for ball in range(turned_ref.shape[0]):
        turned_ref[ball] = kv_ref[ball * BALL : (ball + 1) * BALL, :].T


def pick_turned(ref, listed, first, half):
    return jnp.concatenate([ref[i, first : first + half, :] for i in listed], axis=1)


def combine(turned, weights):
    both = dot(turned, weights, ((1,), (1,)))
    rows, features = both.shape[1] // 2, both.shape[0] // 2
    return jnp.concatenate([both[:features, :rows], both[features:, rows:]], axis=0).T


def in_stages(count, *stages):
    held = {}
    for step in range(count + len(stages) - 1):
        for depth, stage in enumerate(stages):
            ball = step - depth
            if 0 <= ball < count:
                held[ball] = stage(ball, *held.pop(ball, ()))


def softmax_parts(scores):
    exponent = jnp.exp(scores - jnp.max(scores, axis=-1, keepdims=True))
    return exponent, 1.0 / jnp.sum(exponent, axis=-1, keepdims=True)


def backward_stages(lists, core, q_ref, kv_ref, turned_ref, mg_ref, mixed_ref, grads_ref, dk_ref, dv_ref, forward):
    half = q_ref.shape[1]
    scale = (half // 2) ** (-0.5)

    def products(ball):
        at = slice(ball * BALL, (ball + 1) * BALL)
        listed = listed_balls(ball, *lists, core)
        stacked, grad = stack_heads(q_ref[at, :]), stack_heads(mg_ref[at, :])
        scores = dot(stacked, pick(kv_ref, listed, 0, half), ((1,), (1,)))
        weights_grad = dot(grad, pick(kv_ref, listed, half, half), ((1,), (1,)))
        return listed, stacked, grad, scores, weights_grad

    def elements(ball, listed, stacked, grad, scores, weights_grad):
        exponent, inverse = softmax_parts(scores)
        attention = exponent * inverse
        if forward:
            inner = jnp.sum(attention * weights_grad, axis=-1, keepdims=True)
        else:
            mixed = mixed_ref[ball * BALL : (ball + 1) * BALL, :].astype(F32)
            inner = jnp.sum(grad.astype(F32) * jnp.concatenate([mixed, mixed], axis=0), axis=-1, keepdims=True)
        scores_grad = attention * (weights_grad - inner)
        return listed, stacked, grad, attention.astype(BF), scores_grad.astype(BF)

    def gradients(ball, listed, stacked, grad, attention, scores_grad):
        at = slice(ball * BALL, (ball + 1) * BALL)
        if forward:
            mixed_ref[at, :] = combine(pick_turned(turned_ref, listed, half, half), attention).astype(BF)
        queries_grad = combine(pick_turned(turned_ref, listed, 0, half), scores_grad) * scale
        grads_ref[at, :half] = queries_grad.astype(BF)
        add_listed(dk_ref, listed, dot(stacked, scores_grad, ((0,), (0,))))
        add_listed(dv_ref, listed, dot(grad, attention, ((0,), (0,))))
        return ()

    turn_balls(turned_ref, kv_ref)
    dk_ref[...] = jnp.zeros_like(dk_ref)
    dv_ref[...] = jnp.zeros_like(dv_ref)
    in_stages(q_ref.shape[0] // BALL, products, elements, gradients)


def add_listed(ref, listed, part):
    for j, i in enumerate(listed):
        ref[i] += part[:, j * BALL : (j + 1) * BALL]


def normed_grads(grads_ref, dk_ref, dv_ref, columns, store):
    half = dk_ref.shape[1]

    def turn(chunk):
        for ball in range(chunk * CHUNK // BALL, (chunk + 1) * CHUNK // BALL):
            at = slice(ball * BALL, (ball + 1) * BALL)
            grads_ref[at, half : 2 * half] = dk_ref[ball].T.astype(BF)
            grads_ref[at, 2 * half :] = dv_ref[ball].T.astype(BF)
        return ()

    def multiply(chunk):
        at = slice(chunk * CHUNK, (chunk + 1) * CHUNK)
        store(at, dot(grads_ref[at, :], columns, ((1,), (1,))))
        return ()

    in_stages(grads_ref.shape[0] // CHUNK, turn, multiply)


def geo_bit(bit):
    return lax.rem(lax.axis_index("geo") // bit, 2)


def kept(side, quartered):
    half = geo_bit(jnp.where(side == 0, 2, 1))
    return half, geo_bit(jnp.where(side == 0, 1, 2)) if quartered else 0


def store_quarters(ref, blocks, slot):
    size = ref.shape[1]
    ref[slot] = blocks[:size]
    ref[1 - slot] = blocks[size:]


def weight_part(part, normed_ref, grads, mixed, grad_out_ref):
    half = mixed.shape[1]
    weight = dot(normed_ref[:, part_of(part, half)], grads, ((0,), (0,)))
    out = dot(mixed, grad_out_ref[:, part_of(part, half)], ((0,), (0,)))
    blocks = [weight[:, i * half : (i + 1) * half] for i in range(3)] + [out]
    return jnp.concatenate(blocks, axis=0).astype(BF)


def norm_backward(normed_grad, x, gain, grad_out):
    factor = norm_factor(x)
    scaled = normed_grad.astype(BF).astype(F32) * gain
    inner = jnp.mean(scaled * x, axis=-1, keepdims=True)
    return (grad_out.astype(F32) + factor * scaled - x * (factor * factor * factor) * inner).astype(BF)


def norm_project(rows_count, rows_of, gain, columns, normed_ref, q_ref, kv_ref, first=0):
    def norm(chunk, x):
        return ((x * norm_factor(x) * gain).astype(BF),)

    def store(chunk, normed):
        at = slice(first + chunk * CHUNK, first + (chunk + 1) * CHUNK)
        normed_ref[at], (q_ref[at], kv_ref[at]) = normed, project(normed, columns)
        return ()

    in_stages(rows_count // CHUNK, lambda chunk: (rows_of(slice(chunk * CHUNK, (chunk + 1) * CHUNK)),), norm, store)


def project_mine(
    x_hbm, grad_hbm, rot_hbm, lists_one_hbm, lists_two_hbm, gain_one_hbm, gain_two_hbm, qkv_one_hbm, qkv_two_hbm, out_one_hbm, out_two_hbm,
    x, grad, rot, lists_one, lists_two, gain_one, gain_two, qkv_one, qkv_two, out_one, out_two,
    normed_ref, q_ref, kv_ref, sems,
):
    side = own_side()
    half = x.shape[1] // 2
    copies = []

    def start(source, target):
        copies.append(pltpu.make_async_copy(source, target, sems.at[len(copies)]))
        copies[-1].start()

    def start_columns(source, target):
        for i in range(3):
            start(source.at[:, part_of(2 * i + side, half)], target.at[:, i * half : (i + 1) * half])

    start(x_hbm, x)
    start(gain_one_hbm, gain_one)
    start_columns(qkv_one_hbm, qkv_one)
    first = len(copies)
    start(grad_hbm, grad)
    start(rot_hbm, rot)
    start(lists_one_hbm, lists_one)
    start(lists_two_hbm, lists_two)
    start(gain_two_hbm, gain_two)
    start_columns(qkv_two_hbm, qkv_two)
    for source, target in ((out_one_hbm, out_one), (out_two_hbm, out_two)):
        start(source.at[part_of(side, half)], target.at[:half])
        start(source.at[part_of(1 - side, half)], target.at[half:])
    for copy in copies[:first]:
        copy.wait()
    norm_project(
        x.shape[0], lambda at: x[at].astype(F32), gain_row(gain_one), qkv_one[...], normed_ref, q_ref, kv_ref
    )
    for copy in copies[first:]:
        copy.wait()


def first_forward(
    mine, other, x_other, gain, columns, normed_mine, q_mine, kv_mine, mixed_ref, q_ref, kv_ref, normed_ref
):
    core = lax.axis_index("pts")
    local, width = x_other.shape
    half = width // 2
    normed_ref[:local], q_ref[:local], kv_ref[:local] = normed_mine[...], q_mine[...], kv_mine[...]
    norm_project(
        local, lambda at: x_other[at].astype(F32), gain_row(gain), columns[...], normed_ref, q_ref, kv_ref, local
    )

    def products(ball):
        listed = listed_balls(ball, mine, other, core)
        stacked = stack_heads(q_ref[ball * BALL : (ball + 1) * BALL, :])
        return listed, dot(stacked, pick(kv_ref, listed, 0, half), ((1,), (1,)))

    def elements(ball, listed, scores):
        exponent, inverse = softmax_parts(scores)
        return listed, exponent.astype(BF), inverse

    def outputs(ball, listed, exponent, inverse):
        mixed = unstack_heads(dot(exponent, pick(kv_ref, listed, half, half)) * inverse)
        mixed_ref[ball * BALL : (ball + 1) * BALL, :] = mixed.astype(BF)
        return ()

    in_stages(2 * local // BALL, products, elements, outputs)


def before_second(
    rot_mine, rot_other, x_mine, x_other, mixed, grad_mine, grad_other, out_one, out_two,
    base_ref, chosen_ref, chosen_back, grad_ref, mg_ref,
):
    core = lax.axis_index("pts")
    local, width = x_mine.shape
    half = width // 2
    total = 2 * local
    own = out_one[:half]
    base_ref[:local] = x_mine[...].astype(F32) + dot(mixed[:local], own)
    base_ref[local:] = x_other[...].astype(F32) + dot(mixed[local:], own)
    grad_ref[:local] = grad_mine[...]
    grad_ref[local:] = grad_other[...]
    mg_ref[...] = dot(grad_ref[...], out_two[:half], ((1,), (1,))).astype(BF)
    lane = lax.broadcasted_iota(jnp.int32, (BALL, total), 1)
    lane = lax.rem(lane + core * local, total).astype(F32)
    for side, ref in enumerate((rot_mine, rot_other)):
        for j in range(local // BALL):
            row = ref[j : j + 1, :].astype(F32)
            column = jnp.broadcast_to(row, (BALL, BALL)).T[:, :1]
            first = side * local + j * BALL
            chosen_ref[first : first + BALL, :] = (lane == column).astype(BF)
    row_of = [ref[j : j + 1, :] for ref in (rot_mine, rot_other) for j in range(local // BALL)]
    order = lax.rem(jnp.concatenate(row_of, axis=1) + core * local, total)
    place = lax.broadcasted_iota(jnp.int32, (BALL, total), 0)
    for first in range(0, total, BALL):
        chosen_back[first : first + BALL, :] = (place == order - first).astype(BF)


def second_layer(
    mine, other, base, mixed_other, chosen, mg_ref, out_one, gain, columns,
    moved_ref, normed_ref, mixed_ref, mixed_send, grads_ref, part_ref,
    hidden_ref, q_ref, kv_ref, turned_ref, dk_ref, dv_ref,
):
    core = lax.axis_index("pts")
    total, width = base.shape
    local = total // 2
    half = width // 2
    far = out_one[half:]
    for first in range(0, total, CHUNK):
        other_first = (first + local) % total
        added = dot(mixed_other[other_first : other_first + CHUNK], far)
        hidden_ref[first : first + CHUNK] = (base[first : first + CHUNK] + added).astype(BF)

    def rotate(at):
        moved = dot(chosen[at], hidden_ref[...])
        moved_ref[at] = moved.astype(BF)
        return moved

    norm_project(total, rotate, gain_row(gain), columns[...], normed_ref, q_ref, kv_ref)
    backward_stages((mine, other), core, q_ref, kv_ref, turned_ref, mg_ref, mixed_ref, grads_ref, dk_ref, dv_ref, True)

    def store(at, part):
        part_ref[at] = part.astype(BF)

    normed_grads(grads_ref, dk_ref, dv_ref, columns[...], store)
    mixed_send[...] = mixed_ref[local:]


def second_weights(normed, grads, mixed, grad, keep_ref, send_ref):
    part, slot = kept(own_side(), QUARTERED[1])
    store_quarters(send_ref, weight_part(1 - part, normed, grads[...], mixed[...], grad), slot)
    store_quarters(keep_ref, weight_part(part, normed, grads[...], mixed[...], grad), slot)


def first_backward(
    mine, other, chosen_back, part_mine, part_other, moved, grad, gain_two,
    mixed_ref, normed, q_ref, kv_ref, out_one, columns,
    hg_ref, grads_ref, send_ref, part_keep, part_send,
    rows_grad_ref, mg_ref, turned_ref, dk_ref, dv_ref,
):
    core = lax.axis_index("pts")
    total, width = grad.shape
    local = total // 2
    half = width // 2
    gain = gain_row(gain_two)
    for first, far in ((0, local), (local, 0)):
        at = slice(first, first + local)
        normed_grad = part_mine[at].astype(F32) + part_other[far : far + local].astype(F32)
        rows_grad_ref[at] = norm_backward(normed_grad, moved[at].astype(F32), gain, grad[at])

    def rotate(chunk):
        return (dot(chosen_back[chunk * CHUNK : (chunk + 1) * CHUNK], rows_grad_ref[...]).astype(BF),)

    def project_back(chunk, hidden_grad):
        at = slice(chunk * CHUNK, (chunk + 1) * CHUNK)
        hg_ref[at] = hidden_grad
        mg_ref[at] = dot(hidden_grad, out_one[:half], ((1,), (1,))).astype(BF)
        return ()

    in_stages(total // CHUNK, rotate, project_back)
    backward_stages((mine, other), core, q_ref, kv_ref, turned_ref, mg_ref, mixed_ref, grads_ref, dk_ref, dv_ref, False)

    def store(at, part):
        if at.start < local:
            part_keep[at] = part
        else:
            part_send[at.start - local : at.stop - local] = part.astype(BF)

    normed_grads(grads_ref, dk_ref, dv_ref, columns[...], store)
    part, slot = kept(own_side(), QUARTERED[0])
    store_quarters(send_ref, weight_part(1 - part, normed, grads_ref[...], mixed_ref[...], hg_ref), slot)


def finish_rows(
    normed, grads, mixed, hidden_grad, part_mine, part_other, x_mine, gain, moved, mixed_two, mixed_two_other, out_two,
    keep_ref, points_grad, result,
):
    local = x_mine.shape[0]
    part, slot = kept(own_side(), QUARTERED[0])
    store_quarters(keep_ref, weight_part(part, normed, grads[...], mixed[...], hidden_grad), slot)
    normed_grad = part_mine[...] + part_other[...].astype(F32)
    points_grad[...] = norm_backward(
        normed_grad, x_mine[...].astype(F32), gain_row(gain), hidden_grad[:local]
    )
    both = jnp.concatenate([mixed_two[:local], mixed_two_other[...]], axis=1)
    result[...] = (moved[:local].astype(F32) + dot(both, out_two[...])).astype(BF)


def finish_weights(
    quartered, near_mine, far_mine, near_other, far_other, gain, weight, gain_grad, qkv_grad, out_grad, folded_ref
):
    own = own_side()
    size, half = near_mine.shape[1:]
    for side, near, far in ((own, near_mine, far_mine), (1 - own, near_other, far_other)):
        bit, slot = kept(side, quartered)
        for part, ref in ((bit, near), (1 - bit, far)):

            def block(p):
                first = p * half
                quarter = slot if first < size else 1 - slot
                return ref[quarter, first % size : first % size + half].astype(F32)

            at = part_of(part, half)
            folded = jnp.zeros((half, half), F32)
            for p in range(3):
                columns = part_of(2 * p + side, half)
                qkv_grad[at, columns] = block(p)
                folded = folded + block(p) * weight[at, columns].astype(F32)
            folded_ref[side, at] = folded
            out_grad[part_of(side, half), at] = block(3)
    folded = folded_ref[0] + folded_ref[1]
    gain_grad[...] = jnp.sum(folded.T, axis=0, keepdims=True) / gain_row(gain)


def shape(*dims, dtype=BF):
    return jax.ShapeDtypeStruct(dims, dtype)


def call(body, ins, outs, scratch=(), lists=()):
    return pl.pallas_call(
        body,
        name=getattr(body, "func", body).__name__,
        out_shape=outs,
        in_specs=[SMEM] * len(lists) + [VMEM] * len(ins),
        out_specs=[VMEM] * len(outs),
        scratch_shapes=[pltpu.VMEM(item.shape, item.dtype) for item in scratch],
        compiler_params=PARAMS,
    )(*lists, *ins)


def add(a, b):
    return (a.astype(F32) + b.astype(F32)).astype(BF)


def local(
    geo,
    points,
    result_grad,
    lists_one,
    lists_two,
    rotation,
    gain_one,
    qkv_one,
    out_one,
    gain_two,
    qkv_two,
    out_two,
):
    rows, width = points.shape[1:]
    half = width // 2
    total = 2 * rows
    balls = total // BALL
    thin, wide, triple = shape(total, half), shape(total, width), shape(total, 3 * half)
    turned = shape(balls, width, BALL)
    blocks = shape(balls, half, BALL, dtype=F32)
    weights = shape(2, width, half)

    def swap(array):
        return lax.ppermute(array, "pts", SWAP)

    def across(array, bits):
        def place(side, index):
            return (side ^ parity(index)) * geo + index

        pairs = [(place(side, i), place(side, i ^ bit)) for side, bit in enumerate(bits) for i in range(geo)]
        return lax.ppermute(array, ("pts", "geo"), pairs)

    ups = [1 << i for i in range(2, geo.bit_length() - 1)]
    doublings = [(1, 2)] + list(zip(ups, ups[1:] + ups[:1]))

    x = points[0]
    grad = result_grad[0]
    rot = rotation.reshape(rows // BALL, BALL)
    others = [swap(a) for a in (x, lists_one, lists_two, rot, grad)]
    arguments = (x, grad, rot, lists_one, lists_two, gain_one, gain_two, qkv_one, qkv_two, out_one, out_two)
    own_rows = shape(rows, width)
    own_columns = shape(width, 3 * half)
    square = shape(width, width)
    x, grad, rot, *mine, near_gain, far_gain, columns_one, columns_two, out_one, out_two, normed, q, kv = pl.pallas_call(
        project_mine,
        name="project_mine",
        out_shape=[shape(*a.shape, dtype=a.dtype) for a in arguments[:7]]
        + [own_columns, own_columns, square, square, own_rows, shape(rows, half), own_rows],
        in_specs=[HBM] * len(arguments),
        out_specs=[VMEM] * 14,
        scratch_shapes=[pltpu.SemaphoreType.DMA((17,))],
        compiler_params=PARAMS,
    )(*[pltpu.with_memory_space_constraint(a, pltpu.HBM) for a in arguments])
    x_other, one_other, two_other, rot_other, grad_other = lax.optimization_barrier(others)
    one = [mine[0], one_other]
    two = [mine[1], two_other]
    mixed, q, kv, normed = call(
        first_forward, [x_other, near_gain, columns_one, normed, q, kv], [thin, thin, wide, wide], lists=one
    )
    mixed_other = swap(mixed)
    base, chosen, chosen_back, grads_in, mg = call(
        before_second,
        [rot, rot_other, x, x_other, mixed, grad, grad_other, out_one, out_two],
        [shape(total, width, dtype=F32), shape(total, total), shape(total, total), wide, thin],
    )
    moved, normed_two, mixed_two, mixed_send, grads_two, part_two = call(
        second_layer,
        [base, mixed_other, chosen, mg, out_one, far_gain, columns_two],
        [wide, wide, thin, shape(rows, half), triple, wide],
        [wide, thin, wide, turned, blocks, blocks],
        two,
    )
    part_two_other = swap(part_two)
    mixed_two_other = swap(mixed_send)
    keep_two, send_two = call(second_weights, [normed_two, grads_two, mixed_two, grads_in], [weights, weights])
    received_two = across(send_two, (2, 1))
    hidden_grad, grads_one, send, part_keep, part_send = call(
        first_backward,
        [chosen_back, part_two, part_two_other, moved, grads_in, far_gain, mixed, normed, q, kv, out_one, columns_one],
        [wide, triple, weights, shape(rows, width, dtype=F32), own_rows],
        [wide, thin, turned, blocks, blocks],
        one,
    )
    received_two, send = lax.optimization_barrier((received_two, send))
    summed_two = add(keep_two, received_two)
    part_other = swap(part_send)
    received = across(send, (2, 1))
    keep, points_grad, result = call(
        finish_rows,
        [normed, grads_one, mixed, hidden_grad, part_keep, part_other, x, near_gain]
        + [moved, mixed_two, mixed_two_other, out_two],
        [weights, own_rows, own_rows],
    )
    summed = add(keep, received)

    first, rest = doublings[0], doublings[1:]

    def second_step(array, quartered):
        return add(array[:1], across(array[1:], first)) if quartered else add(array, across(array, first))

    summed_two = second_step(summed_two, QUARTERED[1])
    summed = second_step(summed, QUARTERED[0])
    for bits in rest:
        summed_two = add(summed_two, across(summed_two, bits))
        summed = add(summed, across(summed, bits))

    def widen(array, quartered):
        return jnp.concatenate([array, across(array, first)], axis=0) if quartered else array

    summed_two = widen(summed_two, QUARTERED[1])
    summed = widen(summed, QUARTERED[0])
    far_two = across(summed_two, (2, 1))
    far = across(summed, (2, 1))
    tied_two, tied_far_two, _ = lax.optimization_barrier((summed_two, far_two, summed))
    pieces_two = [summed_two, far_two, swap(tied_two), swap(tied_far_two)]
    pieces_one = [summed, far, swap(summed), swap(far)]
    grads = []
    for quartered, pieces, gain, weight in (
        (QUARTERED[0], pieces_one, near_gain, qkv_one),
        (QUARTERED[1], pieces_two, far_gain, qkv_two),
    ):
        found = call(
            functools.partial(finish_weights, quartered),
            pieces + [gain, weight],
            [shape(*dims, dtype=F32) for dims in ((1, width), (width, 3 * width), (width, width))],
            [shape(2, width, half, dtype=F32)],
        )
        grads += [found[0].reshape(width), found[1], found[2]]
    return (result[None], points_grad[None], *grads)


def solution(mesh):
    rows = P("geo", "pts", None)
    placed = (rows,) * 4 + (P("geo", "pts"),) + (P(),) * 6
    return jax.shard_map(
        functools.partial(local, mesh.shape["geo"]),
        mesh=mesh,
        in_specs=placed,
        out_specs=(rows, rows) + (P(),) * 6,
        check_vma=False,
    )
```

```python
import functools

import jax
import jax.numpy as jnp
from jax import lax
from jax.experimental import pallas as pl
from jax.experimental.pallas import tpu as pltpu
from jax.sharding import PartitionSpec as P

HEADS = 4
BALL = 128
LISTED = 4
CHUNK = 512
QUARTERED = (True, True)
EPSILON = 1e-06
BF = jnp.bfloat16
F32 = jnp.float32
SWAP = ((0, 1), (1, 0))

VMEM = pl.BlockSpec(memory_space=pltpu.VMEM)
SMEM = pl.BlockSpec(memory_space=pltpu.SMEM)
HBM = pl.BlockSpec(memory_space=pltpu.HBM)
PARAMS = pltpu.CompilerParams(vmem_limit_bytes=40 * 1024 * 1024)


def dot(a, b, dims=((1,), (0,))):
    return lax.dot_general(a, b, (dims, ((), ())), preferred_element_type=F32)


def norm_factor(x):
    return lax.rsqrt(jnp.mean(x * x, axis=-1, keepdims=True) + EPSILON)


def parity(index):
    for shift in (8, 4, 2, 1):
        index = index ^ (index >> shift)
    return index & 1


def own_side():
    return lax.axis_index("pts") ^ parity(lax.axis_index("geo"))


def part_of(place, size):
    return pl.ds(pl.multiple_of(place * size, size), size)


def gain_row(gain):
    return gain[...].astype(F32).reshape(1, gain.shape[0])


def project(normed, columns):
    qkv = dot(normed, columns)
    half = columns.shape[1] // 3
    scale = (2 * half // HEADS) ** (-0.5)
    return qkv[:, :half].astype(BF) * BF(scale), qkv[:, half:].astype(BF)


def stack_heads(rows):
    lane = lax.broadcasted_iota(jnp.int32, rows.shape, 1)
    first = lane < rows.shape[1] // 2
    zero = jnp.zeros_like(rows)
    return jnp.concatenate([jnp.where(first, rows, zero), jnp.where(first, zero, rows)], axis=0)


def unstack_heads(stacked):
    rows = stacked.shape[0] // 2
    lane = lax.broadcasted_iota(jnp.int32, (rows, stacked.shape[1]), 1)
    return jnp.where(lane < stacked.shape[1] // 2, stacked[:rows], stacked[rows:])


def listed_balls(ball, mine, other, core):
    local_balls = mine.shape[1]
    lists, row = (mine, ball) if ball < local_balls else (other, ball - local_balls)
    return [lax.rem(lists[0, row, j] + core * local_balls, 2 * local_balls) for j in range(LISTED)]


def pick(ref, listed, first, half):
    return jnp.concatenate([ref[part_of(i, BALL), first : first + half] for i in listed], axis=0)


def turn_balls(turned_ref, kv_ref):
    for ball in range(turned_ref.shape[0]):
        turned_ref[ball] = kv_ref[ball * BALL : (ball + 1) * BALL, :].T


def pick_turned(ref, listed, first, half):
    return jnp.concatenate([ref[i, first : first + half, :] for i in listed], axis=1)


def combine(turned, weights):
    both = dot(turned, weights, ((1,), (1,)))
    rows, features = both.shape[1] // 2, both.shape[0] // 2
    return jnp.concatenate([both[:features, :rows], both[features:, rows:]], axis=0).T


def in_stages(count, *stages):
    held = {}
    for step in range(count + len(stages) - 1):
        for depth, stage in enumerate(stages):
            ball = step - depth
            if 0 <= ball < count:
                held[ball] = stage(ball, *held.pop(ball, ()))


def softmax_parts(scores):
    exponent = jnp.exp(scores - jnp.max(scores, axis=-1, keepdims=True))
    return exponent, 1.0 / jnp.sum(exponent, axis=-1, keepdims=True)


def backward_stages(
    lists, core, q_ref, kv_ref, turned_ref, mg_ref, mixed_ref, grads_ref, dk_ref, dv_ref, attention_ref=None
):
    forward = attention_ref is None
    half = q_ref.shape[1]
    scale = (half // 2) ** (-0.5)

    def products(ball):
        at = slice(ball * BALL, (ball + 1) * BALL)
        listed = listed_balls(ball, *lists, core)
        stacked, grad = stack_heads(q_ref[at, :]), stack_heads(mg_ref[at, :])
        scores = dot(stacked, pick(kv_ref, listed, 0, half), ((1,), (1,))) if forward else None
        weights_grad = dot(grad, pick(kv_ref, listed, half, half), ((1,), (1,)))
        return listed, stacked, grad, scores, weights_grad

    def elements(ball, listed, stacked, grad, scores, weights_grad):
        if forward:
            exponent, inverse = softmax_parts(scores)
            attention = exponent * inverse
            inner = jnp.sum(attention * weights_grad, axis=-1, keepdims=True)
        else:
            attention = attention_ref[ball].astype(F32)
            mixed = mixed_ref[ball * BALL : (ball + 1) * BALL, :].astype(F32)
            inner = jnp.sum(grad.astype(F32) * jnp.concatenate([mixed, mixed], axis=0), axis=-1, keepdims=True)
        scores_grad = attention * (weights_grad - inner)
        return listed, stacked, grad, attention.astype(BF), scores_grad.astype(BF)

    def gradients(ball, listed, stacked, grad, attention, scores_grad):
        at = slice(ball * BALL, (ball + 1) * BALL)
        if forward:
            mixed_ref[at, :] = combine(pick_turned(turned_ref, listed, half, half), attention).astype(BF)
        queries_grad = combine(pick_turned(turned_ref, listed, 0, half), scores_grad) * scale
        grads_ref[at, :half] = queries_grad.astype(BF)
        add_listed(dk_ref, listed, dot(stacked, scores_grad, ((0,), (0,))))
        add_listed(dv_ref, listed, dot(grad, attention, ((0,), (0,))))
        return ()

    turn_balls(turned_ref, kv_ref)
    dk_ref[...] = jnp.zeros_like(dk_ref)
    dv_ref[...] = jnp.zeros_like(dv_ref)
    in_stages(q_ref.shape[0] // BALL, products, elements, gradients)


def add_listed(ref, listed, part):
    for j, i in enumerate(listed):
        ref[i] += part[:, j * BALL : (j + 1) * BALL]


def normed_grads(grads_ref, dk_ref, dv_ref, columns, store):
    half = dk_ref.shape[1]

    def turn(chunk):
        for ball in range(chunk * CHUNK // BALL, (chunk + 1) * CHUNK // BALL):
            at = slice(ball * BALL, (ball + 1) * BALL)
            grads_ref[at, half : 2 * half] = dk_ref[ball].T.astype(BF)
            grads_ref[at, 2 * half :] = dv_ref[ball].T.astype(BF)
        return ()

    def multiply(chunk):
        at = slice(chunk * CHUNK, (chunk + 1) * CHUNK)
        store(at, dot(grads_ref[at, :], columns, ((1,), (1,))))
        return ()

    in_stages(grads_ref.shape[0] // CHUNK, turn, multiply)


def geo_bit(bit):
    return lax.rem(lax.axis_index("geo") // bit, 2)


def kept(side, quartered):
    half = geo_bit(jnp.where(side == 0, 2, 1))
    return half, geo_bit(jnp.where(side == 0, 1, 2)) if quartered else 0


def store_quarters(ref, blocks, slot):
    size = ref.shape[1]
    ref[slot] = blocks[:size]
    ref[1 - slot] = blocks[size:]


def weight_part(part, normed_ref, grads, mixed, grad_out_ref):
    half = mixed.shape[1]
    weight = dot(normed_ref[:, part_of(part, half)], grads, ((0,), (0,)))
    out = dot(mixed, grad_out_ref[:, part_of(part, half)], ((0,), (0,)))
    blocks = [weight[:, i * half : (i + 1) * half] for i in range(3)] + [out]
    return jnp.concatenate(blocks, axis=0).astype(BF)


def norm_backward(normed_grad, x, gain, grad_out):
    factor = norm_factor(x)
    scaled = normed_grad.astype(BF).astype(F32) * gain
    inner = jnp.mean(scaled * x, axis=-1, keepdims=True)
    return (grad_out.astype(F32) + factor * scaled - x * (factor * factor * factor) * inner).astype(BF)


def norm_project(rows_count, rows_of, gain, columns, normed_ref, q_ref, kv_ref, first=0):
    def norm(chunk, x):
        return ((x * norm_factor(x) * gain).astype(BF),)

    def store(chunk, normed):
        at = slice(first + chunk * CHUNK, first + (chunk + 1) * CHUNK)
        normed_ref[at], (q_ref[at], kv_ref[at]) = normed, project(normed, columns)
        return ()

    in_stages(rows_count // CHUNK, lambda chunk: (rows_of(slice(chunk * CHUNK, (chunk + 1) * CHUNK)),), norm, store)


def project_mine(
    x_hbm, grad_hbm, rot_hbm, lists_one_hbm, lists_two_hbm, gain_one_hbm, gain_two_hbm, qkv_one_hbm, qkv_two_hbm, out_one_hbm, out_two_hbm,
    x, grad, rot, lists_one, lists_two, gain_one, gain_two, qkv_one, qkv_two, out_one, out_two,
    normed_ref, q_ref, kv_ref, sems,
):
    side = own_side()
    half = x.shape[1] // 2
    copies = []

    def start(source, target):
        copies.append(pltpu.make_async_copy(source, target, sems.at[len(copies)]))
        copies[-1].start()

    def start_columns(source, target):
        for i in range(3):
            start(source.at[:, part_of(2 * i + side, half)], target.at[:, i * half : (i + 1) * half])

    start(x_hbm, x)
    start(gain_one_hbm, gain_one)
    start_columns(qkv_one_hbm, qkv_one)
    first = len(copies)
    start(grad_hbm, grad)
    start(rot_hbm, rot)
    start(lists_one_hbm, lists_one)
    start(lists_two_hbm, lists_two)
    start(gain_two_hbm, gain_two)
    start_columns(qkv_two_hbm, qkv_two)
    for source, target in ((out_one_hbm, out_one), (out_two_hbm, out_two)):
        start(source.at[part_of(side, half)], target.at[:half])
        start(source.at[part_of(1 - side, half)], target.at[half:])
    for copy in copies[:first]:
        copy.wait()
    norm_project(
        x.shape[0], lambda at: x[at].astype(F32), gain_row(gain_one), qkv_one[...], normed_ref, q_ref, kv_ref
    )
    for copy in copies[first:]:
        copy.wait()


def first_forward(
    mine, other, x_other, gain, columns, normed_mine, q_mine, kv_mine, mixed_ref, q_ref, kv_ref, normed_ref,
    attention_ref,
):
    core = lax.axis_index("pts")
    local, width = x_other.shape
    half = width // 2
    normed_ref[:local], q_ref[:local], kv_ref[:local] = normed_mine[...], q_mine[...], kv_mine[...]
    norm_project(
        local, lambda at: x_other[at].astype(F32), gain_row(gain), columns[...], normed_ref, q_ref, kv_ref, local
    )

    def products(ball):
        listed = listed_balls(ball, mine, other, core)
        stacked = stack_heads(q_ref[ball * BALL : (ball + 1) * BALL, :])
        return listed, dot(stacked, pick(kv_ref, listed, 0, half), ((1,), (1,)))

    def elements(ball, listed, scores):
        exponent, inverse = softmax_parts(scores)
        attention = (exponent * inverse).astype(BF)
        attention_ref[ball] = attention
        return listed, attention

    def outputs(ball, listed, attention):
        mixed = unstack_heads(dot(attention, pick(kv_ref, listed, half, half)))
        mixed_ref[ball * BALL : (ball + 1) * BALL, :] = mixed.astype(BF)
        return ()

    in_stages(2 * local // BALL, products, elements, outputs)


def before_second(
    rot_mine, rot_other, x_mine, x_other, mixed, grad_mine, grad_other, out_one, out_two,
    base_ref, chosen_ref, chosen_back, grad_ref, mg_ref,
):
    core = lax.axis_index("pts")
    local, width = x_mine.shape
    half = width // 2
    total = 2 * local
    own = out_one[:half]
    base_ref[:local] = x_mine[...].astype(F32) + dot(mixed[:local], own)
    base_ref[local:] = x_other[...].astype(F32) + dot(mixed[local:], own)
    grad_ref[:local] = grad_mine[...]
    grad_ref[local:] = grad_other[...]
    mg_ref[...] = dot(grad_ref[...], out_two[:half], ((1,), (1,))).astype(BF)
    lane = lax.broadcasted_iota(jnp.int32, (BALL, total), 1)
    lane = lax.rem(lane + core * local, total).astype(F32)
    for side, ref in enumerate((rot_mine, rot_other)):
        for j in range(local // BALL):
            row = ref[j : j + 1, :].astype(F32)
            column = jnp.broadcast_to(row, (BALL, BALL)).T[:, :1]
            first = side * local + j * BALL
            chosen_ref[first : first + BALL, :] = (lane == column).astype(BF)
    row_of = [ref[j : j + 1, :] for ref in (rot_mine, rot_other) for j in range(local // BALL)]
    order = lax.rem(jnp.concatenate(row_of, axis=1) + core * local, total)
    place = lax.broadcasted_iota(jnp.int32, (BALL, total), 0)
    for first in range(0, total, BALL):
        chosen_back[first : first + BALL, :] = (place == order - first).astype(BF)


def second_layer(
    mine, other, base, mixed_other, chosen, mg_ref, out_one, gain, columns,
    moved_ref, normed_ref, mixed_ref, mixed_send, grads_ref, part_ref,
    hidden_ref, q_ref, kv_ref, turned_ref, dk_ref, dv_ref,
):
    core = lax.axis_index("pts")
    total, width = base.shape
    local = total // 2
    half = width // 2
    far = out_one[half:]
    for first in range(0, total, CHUNK):
        other_first = (first + local) % total
        added = dot(mixed_other[other_first : other_first + CHUNK], far)
        hidden_ref[first : first + CHUNK] = (base[first : first + CHUNK] + added).astype(BF)

    def rotate(at):
        moved = dot(chosen[at], hidden_ref[...])
        moved_ref[at] = moved.astype(BF)
        return moved

    norm_project(total, rotate, gain_row(gain), columns[...], normed_ref, q_ref, kv_ref)
    backward_stages((mine, other), core, q_ref, kv_ref, turned_ref, mg_ref, mixed_ref, grads_ref, dk_ref, dv_ref)

    def store(at, part):
        part_ref[at] = part.astype(BF)

    normed_grads(grads_ref, dk_ref, dv_ref, columns[...], store)
    mixed_send[...] = mixed_ref[local:]


def second_weights(normed, grads, mixed, grad, keep_ref, send_ref):
    part, slot = kept(own_side(), QUARTERED[1])
    store_quarters(send_ref, weight_part(1 - part, normed, grads[...], mixed[...], grad), slot)
    store_quarters(keep_ref, weight_part(part, normed, grads[...], mixed[...], grad), slot)


def first_backward(
    mine, other, chosen_back, part_mine, part_other, moved, grad, gain_two,
    mixed_ref, normed, q_ref, kv_ref, attention_ref, out_one, columns,
    hg_ref, grads_ref, send_ref, part_keep, part_send,
    rows_grad_ref, mg_ref, turned_ref, dk_ref, dv_ref,
):
    core = lax.axis_index("pts")
    total, width = grad.shape
    local = total // 2
    half = width // 2
    gain = gain_row(gain_two)
    for first, far in ((0, local), (local, 0)):
        at = slice(first, first + local)
        normed_grad = part_mine[at].astype(F32) + part_other[far : far + local].astype(F32)
        rows_grad_ref[at] = norm_backward(normed_grad, moved[at].astype(F32), gain, grad[at])

    def rotate(chunk):
        return (dot(chosen_back[chunk * CHUNK : (chunk + 1) * CHUNK], rows_grad_ref[...]).astype(BF),)

    def project_back(chunk, hidden_grad):
        at = slice(chunk * CHUNK, (chunk + 1) * CHUNK)
        hg_ref[at] = hidden_grad
        mg_ref[at] = dot(hidden_grad, out_one[:half], ((1,), (1,))).astype(BF)
        return ()

    in_stages(total // CHUNK, rotate, project_back)
    backward_stages(
        (mine, other), core, q_ref, kv_ref, turned_ref, mg_ref, mixed_ref, grads_ref, dk_ref, dv_ref, attention_ref
    )

    def store(at, part):
        if at.start < local:
            part_keep[at] = part
        else:
            part_send[at.start - local : at.stop - local] = part.astype(BF)

    normed_grads(grads_ref, dk_ref, dv_ref, columns[...], store)
    part, slot = kept(own_side(), QUARTERED[0])
    store_quarters(send_ref, weight_part(1 - part, normed, grads_ref[...], mixed_ref[...], hg_ref), slot)


def finish_rows(
    normed, grads, mixed, hidden_grad, part_mine, part_other, x_mine, gain, moved, mixed_two, mixed_two_other, out_two,
    keep_ref, points_grad, result,
):
    local = x_mine.shape[0]
    part, slot = kept(own_side(), QUARTERED[0])
    store_quarters(keep_ref, weight_part(part, normed, grads[...], mixed[...], hidden_grad), slot)
    normed_grad = part_mine[...] + part_other[...].astype(F32)
    points_grad[...] = norm_backward(
        normed_grad, x_mine[...].astype(F32), gain_row(gain), hidden_grad[:local]
    )
    both = jnp.concatenate([mixed_two[:local], mixed_two_other[...]], axis=1)
    result[...] = (moved[:local].astype(F32) + dot(both, out_two[...])).astype(BF)


def finish_weights(
    quartered, near_mine, far_mine, near_other, far_other, gain, weight, gain_grad, qkv_grad, out_grad, folded_ref
):
    own = own_side()
    size, half = near_mine.shape[1:]
    for side, near, far in ((own, near_mine, far_mine), (1 - own, near_other, far_other)):
        bit, slot = kept(side, quartered)
        for part, ref in ((bit, near), (1 - bit, far)):

            def block(p):
                first = p * half
                quarter = slot if first < size else 1 - slot
                return ref[quarter, first % size : first % size + half].astype(F32)

            at = part_of(part, half)
            folded = jnp.zeros((half, half), F32)
            for p in range(3):
                columns = part_of(2 * p + side, half)
                qkv_grad[at, columns] = block(p)
                folded = folded + block(p) * weight[at, columns].astype(F32)
            folded_ref[side, at] = folded
            out_grad[part_of(side, half), at] = block(3)
    folded = folded_ref[0] + folded_ref[1]
    gain_grad[...] = jnp.sum(folded.T, axis=0, keepdims=True) / gain_row(gain)


def shape(*dims, dtype=BF):
    return jax.ShapeDtypeStruct(dims, dtype)


def call(body, ins, outs, scratch=(), lists=()):
    return pl.pallas_call(
        body,
        name=getattr(body, "func", body).__name__,
        out_shape=outs,
        in_specs=[SMEM] * len(lists) + [VMEM] * len(ins),
        out_specs=[VMEM] * len(outs),
        scratch_shapes=[pltpu.VMEM(item.shape, item.dtype) for item in scratch],
        compiler_params=PARAMS,
    )(*lists, *ins)


def add(a, b):
    return (a.astype(F32) + b.astype(F32)).astype(BF)


def local(
    geo,
    points,
    result_grad,
    lists_one,
    lists_two,
    rotation,
    gain_one,
    qkv_one,
    out_one,
    gain_two,
    qkv_two,
    out_two,
):
    rows, width = points.shape[1:]
    half = width // 2
    total = 2 * rows
    balls = total // BALL
    thin, wide, triple = shape(total, half), shape(total, width), shape(total, 3 * half)
    turned = shape(balls, width, BALL)
    blocks = shape(balls, half, BALL, dtype=F32)
    weights = shape(2, width, half)

    def swap(array):
        return lax.ppermute(array, "pts", SWAP)

    def across(array, bits):
        def place(side, index):
            return (side ^ parity(index)) * geo + index

        pairs = [(place(side, i), place(side, i ^ bit)) for side, bit in enumerate(bits) for i in range(geo)]
        return lax.ppermute(array, ("pts", "geo"), pairs)

    ups = [1 << i for i in range(2, geo.bit_length() - 1)]
    doublings = [(1, 2)] + list(zip(ups, ups[1:] + ups[:1]))

    x = points[0]
    grad = result_grad[0]
    rot = rotation.reshape(rows // BALL, BALL)
    others = [swap(a) for a in (x, lists_one, lists_two, rot, grad)]
    arguments = (x, grad, rot, lists_one, lists_two, gain_one, gain_two, qkv_one, qkv_two, out_one, out_two)
    own_rows = shape(rows, width)
    own_columns = shape(width, 3 * half)
    square = shape(width, width)
    x, grad, rot, *mine, near_gain, far_gain, columns_one, columns_two, out_one, out_two, normed, q, kv = pl.pallas_call(
        project_mine,
        name="project_mine",
        out_shape=[shape(*a.shape, dtype=a.dtype) for a in arguments[:7]]
        + [own_columns, own_columns, square, square, own_rows, shape(rows, half), own_rows],
        in_specs=[HBM] * len(arguments),
        out_specs=[VMEM] * 14,
        scratch_shapes=[pltpu.SemaphoreType.DMA((17,))],
        compiler_params=PARAMS,
    )(*[pltpu.with_memory_space_constraint(a, pltpu.HBM) for a in arguments])
    x_other, one_other, two_other, rot_other, grad_other = lax.optimization_barrier(others)
    one = [mine[0], one_other]
    two = [mine[1], two_other]
    mixed, q, kv, normed, attention = call(
        first_forward, [x_other, near_gain, columns_one, normed, q, kv], [thin, thin, wide, wide, shape(balls, 2 * BALL, LISTED * BALL)], lists=one
    )
    mixed_other = swap(mixed)
    base, chosen, chosen_back, grads_in, mg = call(
        before_second,
        [rot, rot_other, x, x_other, mixed, grad, grad_other, out_one, out_two],
        [shape(total, width, dtype=F32), shape(total, total), shape(total, total), wide, thin],
    )
    moved, normed_two, mixed_two, mixed_send, grads_two, part_two = call(
        second_layer,
        [base, mixed_other, chosen, mg, out_one, far_gain, columns_two],
        [wide, wide, thin, shape(rows, half), triple, wide],
        [wide, thin, wide, turned, blocks, blocks],
        two,
    )
    part_two_other = swap(part_two)
    mixed_two_other = swap(mixed_send)
    keep_two, send_two = call(second_weights, [normed_two, grads_two, mixed_two, grads_in], [weights, weights])
    received_two = across(send_two, (2, 1))
    hidden_grad, grads_one, send, part_keep, part_send = call(
        first_backward,
        [chosen_back, part_two, part_two_other, moved, grads_in, far_gain, mixed, normed, q, kv, attention]
        + [out_one, columns_one],
        [wide, triple, weights, shape(rows, width, dtype=F32), own_rows],
        [wide, thin, turned, blocks, blocks],
        one,
    )
    received_two, send = lax.optimization_barrier((received_two, send))
    summed_two = add(keep_two, received_two)
    part_other = swap(part_send)
    received = across(send, (2, 1))
    keep, points_grad, result = call(
        finish_rows,
        [normed, grads_one, mixed, hidden_grad, part_keep, part_other, x, near_gain]
        + [moved, mixed_two, mixed_two_other, out_two],
        [weights, own_rows, own_rows],
    )
    summed = add(keep, received)

    first, rest = doublings[0], doublings[1:]

    def second_step(array, quartered):
        return add(array[:1], across(array[1:], first)) if quartered else add(array, across(array, first))

    summed_two = second_step(summed_two, QUARTERED[1])
    summed = second_step(summed, QUARTERED[0])
    for bits in rest:
        summed_two = add(summed_two, across(summed_two, bits))
        summed = add(summed, across(summed, bits))

    def widen(array, quartered):
        return jnp.concatenate([array, across(array, first)], axis=0) if quartered else array

    summed_two = widen(summed_two, QUARTERED[1])
    summed = widen(summed, QUARTERED[0])
    far_two = across(summed_two, (2, 1))
    far = across(summed, (2, 1))
    tied_two, tied_far_two, _ = lax.optimization_barrier((summed_two, far_two, summed))
    pieces_two = [summed_two, far_two, swap(tied_two), swap(tied_far_two)]
    pieces_one = [summed, far, swap(summed), swap(far)]
    grads = []
    for quartered, pieces, gain, weight in (
        (QUARTERED[0], pieces_one, near_gain, qkv_one),
        (QUARTERED[1], pieces_two, far_gain, qkv_two),
    ):
        found = call(
            functools.partial(finish_weights, quartered),
            pieces + [gain, weight],
            [shape(*dims, dtype=F32) for dims in ((1, width), (width, 3 * width), (width, width))],
            [shape(2, width, half, dtype=F32)],
        )
        grads += [found[0].reshape(width), found[1], found[2]]
    return (result[None], points_grad[None], *grads)


def solution(mesh):
    rows = P("geo", "pts", None)
    placed = (rows,) * 4 + (P("geo", "pts"),) + (P(),) * 6
    return jax.shard_map(
        functools.partial(local, mesh.shape["geo"]),
        mesh=mesh,
        in_specs=placed,
        out_specs=(rows, rows) + (P(),) * 6,
        check_vma=False,
    )
```

```python
import functools

import jax
import jax.numpy as jnp
from jax import lax
from jax.experimental import pallas as pl
from jax.experimental.pallas import tpu as pltpu
from jax.sharding import PartitionSpec as P

HEADS = 4
BALL = 128
LISTED = 4
CHUNK = 512
QUARTERED = (True, True)
EPSILON = 1e-06
BF = jnp.bfloat16
F32 = jnp.float32
SWAP = ((0, 1), (1, 0))

VMEM = pl.BlockSpec(memory_space=pltpu.VMEM)
SMEM = pl.BlockSpec(memory_space=pltpu.SMEM)
HBM = pl.BlockSpec(memory_space=pltpu.HBM)
PARAMS = pltpu.CompilerParams(vmem_limit_bytes=40 * 1024 * 1024)


def dot(a, b, dims=((1,), (0,))):
    return lax.dot_general(a, b, (dims, ((), ())), preferred_element_type=F32)


def norm_factor(x):
    return lax.rsqrt(jnp.mean(x * x, axis=-1, keepdims=True) + EPSILON)


def parity(index):
    for shift in (8, 4, 2, 1):
        index = index ^ (index >> shift)
    return index & 1


def own_side():
    return lax.axis_index("pts") ^ parity(lax.axis_index("geo"))


def part_of(place, size):
    return pl.ds(pl.multiple_of(place * size, size), size)


def gain_row(gain):
    return gain[...].astype(F32).reshape(1, gain.shape[0])


def project(normed, columns):
    qkv = dot(normed, columns)
    half = columns.shape[1] // 3
    scale = (2 * half // HEADS) ** (-0.5)
    return qkv[:, :half].astype(BF) * BF(scale), qkv[:, half:].astype(BF)


def stack_heads(rows):
    lane = lax.broadcasted_iota(jnp.int32, rows.shape, 1)
    first = lane < rows.shape[1] // 2
    zero = jnp.zeros_like(rows)
    return jnp.concatenate([jnp.where(first, rows, zero), jnp.where(first, zero, rows)], axis=0)


def unstack_heads(stacked):
    rows = stacked.shape[0] // 2
    lane = lax.broadcasted_iota(jnp.int32, (rows, stacked.shape[1]), 1)
    return jnp.where(lane < stacked.shape[1] // 2, stacked[:rows], stacked[rows:])


def listed_balls(ball, mine, other, core):
    local_balls = mine.shape[1]
    lists, row = (mine, ball) if ball < local_balls else (other, ball - local_balls)
    return [lax.rem(lists[0, row, j] + core * local_balls, 2 * local_balls) for j in range(LISTED)]


def pick(ref, listed, first, half):
    return jnp.concatenate([ref[part_of(i, BALL), first : first + half] for i in listed], axis=0)


def turn_balls(turned_ref, kv_ref):
    for ball in range(turned_ref.shape[0]):
        turned_ref[ball] = kv_ref[ball * BALL : (ball + 1) * BALL, :].T


def pick_turned(ref, listed, first, half):
    return jnp.concatenate([ref[i, first : first + half, :] for i in listed], axis=1)


def combine(turned, weights):
    both = dot(turned, weights, ((1,), (1,)))
    rows, features = both.shape[1] // 2, both.shape[0] // 2
    return jnp.concatenate([both[:features, :rows], both[features:, rows:]], axis=0).T


def in_stages(count, *stages):
    held = {}
    for step in range(count + len(stages) - 1):
        for depth, stage in enumerate(stages):
            ball = step - depth
            if 0 <= ball < count:
                held[ball] = stage(ball, *held.pop(ball, ()))


def softmax_parts(scores):
    exponent = jnp.exp(scores - jnp.max(scores, axis=-1, keepdims=True))
    return exponent, 1.0 / jnp.sum(exponent, axis=-1, keepdims=True)


def forward_stages(lists, core, q_ref, kv_ref, attention_ref, mixed_ref):
    half = q_ref.shape[1]

    def products(ball):
        listed = listed_balls(ball, *lists, core)
        stacked = stack_heads(q_ref[ball * BALL : (ball + 1) * BALL, :])
        return listed, dot(stacked, pick(kv_ref, listed, 0, half), ((1,), (1,)))

    def elements(ball, listed, scores):
        exponent, inverse = softmax_parts(scores)
        attention = (exponent * inverse).astype(BF)
        attention_ref[ball] = attention
        return listed, attention

    def outputs(ball, listed, attention):
        mixed = unstack_heads(dot(attention, pick(kv_ref, listed, half, half)))
        mixed_ref[ball * BALL : (ball + 1) * BALL, :] = mixed.astype(BF)
        return ()

    return products, elements, outputs


def backward_stages(
    lists, core, q_ref, kv_ref, turned_ref, mg_ref, mixed_ref, grads_ref, dk_ref, dv_ref, attention_ref
):
    half = q_ref.shape[1]
    scale = (half // 2) ** (-0.5)

    def products(ball):
        listed = listed_balls(ball, *lists, core)
        grad = stack_heads(mg_ref[ball * BALL : (ball + 1) * BALL, :])
        return listed, grad, dot(grad, pick(kv_ref, listed, half, half), ((1,), (1,)))

    def elements(ball, listed, grad, weights_grad):
        mixed = mixed_ref[ball * BALL : (ball + 1) * BALL, :].astype(F32)
        inner = jnp.sum(grad.astype(F32) * jnp.concatenate([mixed, mixed], axis=0), axis=-1, keepdims=True)
        attention = attention_ref[ball]
        return listed, grad, attention, (attention.astype(F32) * (weights_grad - inner)).astype(BF)

    def gradients(ball, listed, grad, attention, scores_grad):
        at = slice(ball * BALL, (ball + 1) * BALL)
        queries_grad = combine(pick_turned(turned_ref, listed, 0, half), scores_grad) * scale
        grads_ref[at, :half] = queries_grad.astype(BF)
        add_listed(dk_ref, listed, dot(stack_heads(q_ref[at, :]), scores_grad, ((0,), (0,))))
        add_listed(dv_ref, listed, dot(grad, attention, ((0,), (0,))))
        return ()

    turn_balls(turned_ref, kv_ref)
    dk_ref[...] = jnp.zeros_like(dk_ref)
    dv_ref[...] = jnp.zeros_like(dv_ref)
    return products, elements, gradients


def add_listed(ref, listed, part):
    for j, i in enumerate(listed):
        ref[i] += part[:, j * BALL : (j + 1) * BALL]


def normed_grads(grads_ref, dk_ref, dv_ref, columns, store):
    half = dk_ref.shape[1]

    def turn(chunk):
        for ball in range(chunk * CHUNK // BALL, (chunk + 1) * CHUNK // BALL):
            at = slice(ball * BALL, (ball + 1) * BALL)
            grads_ref[at, half : 2 * half] = dk_ref[ball].T.astype(BF)
            grads_ref[at, 2 * half :] = dv_ref[ball].T.astype(BF)
        return ()

    def multiply(chunk):
        at = slice(chunk * CHUNK, (chunk + 1) * CHUNK)
        store(at, dot(grads_ref[at, :], columns, ((1,), (1,))))
        return ()

    in_stages(grads_ref.shape[0] // CHUNK, turn, multiply)


def geo_bit(bit):
    return lax.rem(lax.axis_index("geo") // bit, 2)


def kept(side, quartered):
    half = geo_bit(jnp.where(side == 0, 2, 1))
    return half, geo_bit(jnp.where(side == 0, 1, 2)) if quartered else 0


def store_quarters(ref, blocks, slot):
    size = ref.shape[1]
    ref[slot] = blocks[:size]
    ref[1 - slot] = blocks[size:]


def weight_part(part, normed_ref, grads, mixed, grad_out_ref):
    half = mixed.shape[1]
    weight = dot(normed_ref[:, part_of(part, half)], grads, ((0,), (0,)))
    out = dot(mixed, grad_out_ref[:, part_of(part, half)], ((0,), (0,)))
    blocks = [weight[:, i * half : (i + 1) * half] for i in range(3)] + [out]
    return jnp.concatenate(blocks, axis=0).astype(BF)


def norm_backward(normed_grad, x, gain, grad_out):
    factor = norm_factor(x)
    scaled = normed_grad.astype(BF).astype(F32) * gain
    inner = jnp.mean(scaled * x, axis=-1, keepdims=True)
    return (grad_out.astype(F32) + factor * scaled - x * (factor * factor * factor) * inner).astype(BF)


def norm_project(rows_count, rows_of, gain, columns, normed_ref, q_ref, kv_ref, first=0):
    def norm(chunk, x):
        return ((x * norm_factor(x) * gain).astype(BF),)

    def store(chunk, normed):
        at = slice(first + chunk * CHUNK, first + (chunk + 1) * CHUNK)
        normed_ref[at], (q_ref[at], kv_ref[at]) = normed, project(normed, columns)
        return ()

    in_stages(rows_count // CHUNK, lambda chunk: (rows_of(slice(chunk * CHUNK, (chunk + 1) * CHUNK)),), norm, store)


def project_mine(
    x_hbm, grad_hbm, rot_hbm, lists_one_hbm, lists_two_hbm, gain_one_hbm, gain_two_hbm, qkv_one_hbm, qkv_two_hbm, out_one_hbm, out_two_hbm,
    x, grad, rot, lists_one, lists_two, gain_one, gain_two, qkv_one, qkv_two, out_one, out_two,
    normed_ref, q_ref, kv_ref, sems,
):
    side = own_side()
    half = x.shape[1] // 2
    copies = []

    def start(source, target):
        copies.append(pltpu.make_async_copy(source, target, sems.at[len(copies)]))
        copies[-1].start()

    def start_columns(source, target):
        for i in range(3):
            start(source.at[:, part_of(2 * i + side, half)], target.at[:, i * half : (i + 1) * half])

    start(x_hbm, x)
    start(gain_one_hbm, gain_one)
    start_columns(qkv_one_hbm, qkv_one)
    first = len(copies)
    start(grad_hbm, grad)
    start(rot_hbm, rot)
    start(lists_one_hbm, lists_one)
    start(lists_two_hbm, lists_two)
    start(gain_two_hbm, gain_two)
    start_columns(qkv_two_hbm, qkv_two)
    for source, target in ((out_one_hbm, out_one), (out_two_hbm, out_two)):
        start(source.at[part_of(side, half)], target.at[:half])
        start(source.at[part_of(1 - side, half)], target.at[half:])
    for copy in copies[:first]:
        copy.wait()
    norm_project(
        x.shape[0], lambda at: x[at].astype(F32), gain_row(gain_one), qkv_one[...], normed_ref, q_ref, kv_ref
    )
    for copy in copies[first:]:
        copy.wait()


def first_forward(
    mine, other, x_other, gain, columns, normed_mine, q_mine, kv_mine, mixed_ref, q_ref, kv_ref, normed_ref,
    attention_ref,
):
    core = lax.axis_index("pts")
    local, width = x_other.shape
    half = width // 2
    normed_ref[:local], q_ref[:local], kv_ref[:local] = normed_mine[...], q_mine[...], kv_mine[...]
    norm_project(
        local, lambda at: x_other[at].astype(F32), gain_row(gain), columns[...], normed_ref, q_ref, kv_ref, local
    )
    stages = forward_stages((mine, other), core, q_ref, kv_ref, attention_ref, mixed_ref)
    in_stages(2 * local // BALL, *stages)


def before_second(
    rot_mine, rot_other, x_mine, x_other, mixed, grad_mine, grad_other, out_one, out_two,
    base_ref, chosen_ref, chosen_back, grad_ref, mg_ref,
):
    core = lax.axis_index("pts")
    local, width = x_mine.shape
    half = width // 2
    total = 2 * local
    own = out_one[:half]
    base_ref[:local] = x_mine[...].astype(F32) + dot(mixed[:local], own)
    base_ref[local:] = x_other[...].astype(F32) + dot(mixed[local:], own)
    grad_ref[:local] = grad_mine[...]
    grad_ref[local:] = grad_other[...]
    mg_ref[...] = dot(grad_ref[...], out_two[:half], ((1,), (1,))).astype(BF)
    lane = lax.broadcasted_iota(jnp.int32, (BALL, total), 1)
    lane = lax.rem(lane + core * local, total).astype(F32)
    for side, ref in enumerate((rot_mine, rot_other)):
        for j in range(local // BALL):
            row = ref[j : j + 1, :].astype(F32)
            column = jnp.broadcast_to(row, (BALL, BALL)).T[:, :1]
            first = side * local + j * BALL
            chosen_ref[first : first + BALL, :] = (lane == column).astype(BF)
    row_of = [ref[j : j + 1, :] for ref in (rot_mine, rot_other) for j in range(local // BALL)]
    order = lax.rem(jnp.concatenate(row_of, axis=1) + core * local, total)
    place = lax.broadcasted_iota(jnp.int32, (BALL, total), 0)
    for first in range(0, total, BALL):
        chosen_back[first : first + BALL, :] = (place == order - first).astype(BF)


def second_layer(
    mine, other, base, mixed_other, chosen, mg_ref, out_one, gain, columns,
    moved_ref, normed_ref, mixed_ref, mixed_send, grads_ref, part_ref,
    hidden_ref, q_ref, kv_ref, turned_ref, attention_ref, dk_ref, dv_ref,
):
    core = lax.axis_index("pts")
    total, width = base.shape
    local = total // 2
    half = width // 2
    far = out_one[half:]
    for first in range(0, total, CHUNK):
        other_first = (first + local) % total
        added = dot(mixed_other[other_first : other_first + CHUNK], far)
        hidden_ref[first : first + CHUNK] = (base[first : first + CHUNK] + added).astype(BF)

    def rotate(at):
        moved = dot(chosen[at], hidden_ref[...])
        moved_ref[at] = moved.astype(BF)
        return moved

    norm_project(total, rotate, gain_row(gain), columns[...], normed_ref, q_ref, kv_ref)
    lists = (mine, other)
    forward = forward_stages(lists, core, q_ref, kv_ref, attention_ref, mixed_ref)
    backward = backward_stages(
        lists, core, q_ref, kv_ref, turned_ref, mg_ref, mixed_ref, grads_ref, dk_ref, dv_ref, attention_ref
    )
    in_stages(total // BALL, *forward, *backward)

    def store(at, part):
        part_ref[at] = part.astype(BF)

    normed_grads(grads_ref, dk_ref, dv_ref, columns[...], store)
    mixed_send[...] = mixed_ref[local:]


def second_weights(normed, grads, mixed, grad, keep_ref, send_ref):
    part, slot = kept(own_side(), QUARTERED[1])
    store_quarters(send_ref, weight_part(1 - part, normed, grads[...], mixed[...], grad), slot)
    store_quarters(keep_ref, weight_part(part, normed, grads[...], mixed[...], grad), slot)


def first_backward(
    mine, other, chosen_back, part_mine, part_other, moved, grad, gain_two,
    mixed_ref, normed, q_ref, kv_ref, attention_ref, out_one, columns,
    hg_ref, grads_ref, send_ref, part_keep, part_send,
    rows_grad_ref, mg_ref, turned_ref, dk_ref, dv_ref,
):
    core = lax.axis_index("pts")
    total, width = grad.shape
    local = total // 2
    half = width // 2
    gain = gain_row(gain_two)
    for first, far in ((0, local), (local, 0)):
        at = slice(first, first + local)
        normed_grad = part_mine[at].astype(F32) + part_other[far : far + local].astype(F32)
        rows_grad_ref[at] = norm_backward(normed_grad, moved[at].astype(F32), gain, grad[at])

    def rotate(chunk):
        return (dot(chosen_back[chunk * CHUNK : (chunk + 1) * CHUNK], rows_grad_ref[...]).astype(BF),)

    def project_back(chunk, hidden_grad):
        at = slice(chunk * CHUNK, (chunk + 1) * CHUNK)
        hg_ref[at] = hidden_grad
        mg_ref[at] = dot(hidden_grad, out_one[:half], ((1,), (1,))).astype(BF)
        return ()

    in_stages(total // CHUNK, rotate, project_back)
    stages = backward_stages(
        (mine, other), core, q_ref, kv_ref, turned_ref, mg_ref, mixed_ref, grads_ref, dk_ref, dv_ref, attention_ref
    )
    in_stages(total // BALL, *stages)

    def store(at, part):
        if at.start < local:
            part_keep[at] = part
        else:
            part_send[at.start - local : at.stop - local] = part.astype(BF)

    normed_grads(grads_ref, dk_ref, dv_ref, columns[...], store)
    part, slot = kept(own_side(), QUARTERED[0])
    store_quarters(send_ref, weight_part(1 - part, normed, grads_ref[...], mixed_ref[...], hg_ref), slot)


def finish_rows(
    normed, grads, mixed, hidden_grad, part_mine, part_other, x_mine, gain, moved, mixed_two, mixed_two_other, out_two,
    keep_ref, points_grad, result,
):
    local = x_mine.shape[0]
    part, slot = kept(own_side(), QUARTERED[0])
    store_quarters(keep_ref, weight_part(part, normed, grads[...], mixed[...], hidden_grad), slot)
    normed_grad = part_mine[...] + part_other[...].astype(F32)
    points_grad[...] = norm_backward(
        normed_grad, x_mine[...].astype(F32), gain_row(gain), hidden_grad[:local]
    )
    both = jnp.concatenate([mixed_two[:local], mixed_two_other[...]], axis=1)
    result[...] = (moved[:local].astype(F32) + dot(both, out_two[...])).astype(BF)


def finish_weights(
    quartered, near_mine, far_mine, near_other, far_other, gain, weight, gain_grad, qkv_grad, out_grad, folded_ref
):
    own = own_side()
    size, half = near_mine.shape[1:]
    for side, near, far in ((own, near_mine, far_mine), (1 - own, near_other, far_other)):
        bit, slot = kept(side, quartered)
        for part, ref in ((bit, near), (1 - bit, far)):

            def block(p):
                first = p * half
                quarter = slot if first < size else 1 - slot
                return ref[quarter, first % size : first % size + half].astype(F32)

            at = part_of(part, half)
            folded = jnp.zeros((half, half), F32)
            for p in range(3):
                columns = part_of(2 * p + side, half)
                qkv_grad[at, columns] = block(p)
                folded = folded + block(p) * weight[at, columns].astype(F32)
            folded_ref[side, at] = folded
            out_grad[part_of(side, half), at] = block(3)
    folded = folded_ref[0] + folded_ref[1]
    gain_grad[...] = jnp.sum(folded.T, axis=0, keepdims=True) / gain_row(gain)


def shape(*dims, dtype=BF):
    return jax.ShapeDtypeStruct(dims, dtype)


def call(body, ins, outs, scratch=(), lists=()):
    return pl.pallas_call(
        body,
        name=getattr(body, "func", body).__name__,
        out_shape=outs,
        in_specs=[SMEM] * len(lists) + [VMEM] * len(ins),
        out_specs=[VMEM] * len(outs),
        scratch_shapes=[pltpu.VMEM(item.shape, item.dtype) for item in scratch],
        compiler_params=PARAMS,
    )(*lists, *ins)


def add(a, b):
    return (a.astype(F32) + b.astype(F32)).astype(BF)


def local(
    geo,
    points,
    result_grad,
    lists_one,
    lists_two,
    rotation,
    gain_one,
    qkv_one,
    out_one,
    gain_two,
    qkv_two,
    out_two,
):
    rows, width = points.shape[1:]
    half = width // 2
    total = 2 * rows
    balls = total // BALL
    thin, wide, triple = shape(total, half), shape(total, width), shape(total, 3 * half)
    turned = shape(balls, width, BALL)
    kept_attention = shape(balls, 2 * BALL, LISTED * BALL)
    blocks = shape(balls, half, BALL, dtype=F32)
    weights = shape(2, width, half)

    def swap(array):
        return lax.ppermute(array, "pts", SWAP)

    def across(array, bits):
        def place(side, index):
            return (side ^ parity(index)) * geo + index

        pairs = [(place(side, i), place(side, i ^ bit)) for side, bit in enumerate(bits) for i in range(geo)]
        return lax.ppermute(array, ("pts", "geo"), pairs)

    ups = [1 << i for i in range(2, geo.bit_length() - 1)]
    doublings = [(1, 2)] + list(zip(ups, ups[1:] + ups[:1]))

    x = points[0]
    grad = result_grad[0]
    rot = rotation.reshape(rows // BALL, BALL)
    others = [swap(a) for a in (x, lists_one, lists_two, rot, grad)]
    arguments = (x, grad, rot, lists_one, lists_two, gain_one, gain_two, qkv_one, qkv_two, out_one, out_two)
    own_rows = shape(rows, width)
    own_columns = shape(width, 3 * half)
    square = shape(width, width)
    x, grad, rot, *mine, near_gain, far_gain, columns_one, columns_two, out_one, out_two, normed, q, kv = pl.pallas_call(
        project_mine,
        name="project_mine",
        out_shape=[shape(*a.shape, dtype=a.dtype) for a in arguments[:7]]
        + [own_columns, own_columns, square, square, own_rows, shape(rows, half), own_rows],
        in_specs=[HBM] * len(arguments),
        out_specs=[VMEM] * 14,
        scratch_shapes=[pltpu.SemaphoreType.DMA((17,))],
        compiler_params=PARAMS,
    )(*[pltpu.with_memory_space_constraint(a, pltpu.HBM) for a in arguments])
    x_other, one_other, two_other, rot_other, grad_other = lax.optimization_barrier(others)
    one = [mine[0], one_other]
    two = [mine[1], two_other]
    mixed, q, kv, normed, attention = call(
        first_forward, [x_other, near_gain, columns_one, normed, q, kv], [thin, thin, wide, wide, kept_attention], lists=one
    )
    mixed_other = swap(mixed)
    base, chosen, chosen_back, grads_in, mg = call(
        before_second,
        [rot, rot_other, x, x_other, mixed, grad, grad_other, out_one, out_two],
        [shape(total, width, dtype=F32), shape(total, total), shape(total, total), wide, thin],
    )
    moved, normed_two, mixed_two, mixed_send, grads_two, part_two = call(
        second_layer,
        [base, mixed_other, chosen, mg, out_one, far_gain, columns_two],
        [wide, wide, thin, shape(rows, half), triple, wide],
        [wide, thin, wide, turned, kept_attention, blocks, blocks],
        two,
    )
    part_two_other = swap(part_two)
    mixed_two_other = swap(mixed_send)
    keep_two, send_two = call(second_weights, [normed_two, grads_two, mixed_two, grads_in], [weights, weights])
    received_two = across(send_two, (2, 1))
    hidden_grad, grads_one, send, part_keep, part_send = call(
        first_backward,
        [chosen_back, part_two, part_two_other, moved, grads_in, far_gain, mixed, normed, q, kv, attention]
        + [out_one, columns_one],
        [wide, triple, weights, shape(rows, width, dtype=F32), own_rows],
        [wide, thin, turned, blocks, blocks],
        one,
    )
    received_two, send = lax.optimization_barrier((received_two, send))
    summed_two = add(keep_two, received_two)
    part_other = swap(part_send)
    received = across(send, (2, 1))
    keep, points_grad, result = call(
        finish_rows,
        [normed, grads_one, mixed, hidden_grad, part_keep, part_other, x, near_gain]
        + [moved, mixed_two, mixed_two_other, out_two],
        [weights, own_rows, own_rows],
    )
    summed = add(keep, received)

    first, rest = doublings[0], doublings[1:]

    def second_step(array, quartered):
        return add(array[:1], across(array[1:], first)) if quartered else add(array, across(array, first))

    summed_two = second_step(summed_two, QUARTERED[1])
    summed = second_step(summed, QUARTERED[0])
    for bits in rest:
        summed_two = add(summed_two, across(summed_two, bits))
        summed = add(summed, across(summed, bits))

    def widen(array, quartered):
        return jnp.concatenate([array, across(array, first)], axis=0) if quartered else array

    summed_two = widen(summed_two, QUARTERED[1])
    summed = widen(summed, QUARTERED[0])
    far_two = across(summed_two, (2, 1))
    far = across(summed, (2, 1))
    tied_two, tied_far_two, _ = lax.optimization_barrier((summed_two, far_two, summed))
    pieces_two = [summed_two, far_two, swap(tied_two), swap(tied_far_two)]
    pieces_one = [summed, far, swap(summed), swap(far)]
    grads = []
    for quartered, pieces, gain, weight in (
        (QUARTERED[0], pieces_one, near_gain, qkv_one),
        (QUARTERED[1], pieces_two, far_gain, qkv_two),
    ):
        found = call(
            functools.partial(finish_weights, quartered),
            pieces + [gain, weight],
            [shape(*dims, dtype=F32) for dims in ((1, width), (width, 3 * width), (width, width))],
            [shape(2, width, half, dtype=F32)],
        )
        grads += [found[0].reshape(width), found[1], found[2]]
    return (result[None], points_grad[None], *grads)


def solution(mesh):
    rows = P("geo", "pts", None)
    placed = (rows,) * 4 + (P("geo", "pts"),) + (P(),) * 6
    return jax.shard_map(
        functools.partial(local, mesh.shape["geo"]),
        mesh=mesh,
        in_specs=placed,
        out_specs=(rows, rows) + (P(),) * 6,
        check_vma=False,
    )
```

```python
import functools

import jax
import jax.numpy as jnp
from jax import lax
from jax.experimental import pallas as pl
from jax.experimental.pallas import tpu as pltpu
from jax.sharding import PartitionSpec as P

HEADS = 4
BALL = 128
LISTED = 4
CHUNK = 512
QUARTERED = (True, True)
EPSILON = 1e-06
BF = jnp.bfloat16
F32 = jnp.float32
SWAP = ((0, 1), (1, 0))

VMEM = pl.BlockSpec(memory_space=pltpu.VMEM)
SMEM = pl.BlockSpec(memory_space=pltpu.SMEM)
HBM = pl.BlockSpec(memory_space=pltpu.HBM)
PARAMS = pltpu.CompilerParams(vmem_limit_bytes=40 * 1024 * 1024)


def dot(a, b, dims=((1,), (0,))):
    return lax.dot_general(a, b, (dims, ((), ())), preferred_element_type=F32)


def norm_factor(x):
    return lax.rsqrt(jnp.mean(x * x, axis=-1, keepdims=True) + EPSILON)


def parity(index):
    for shift in (8, 4, 2, 1):
        index = index ^ (index >> shift)
    return index & 1


def own_side():
    return lax.axis_index("pts") ^ parity(lax.axis_index("geo"))


def part_of(place, size):
    return pl.ds(pl.multiple_of(place * size, size), size)


def gain_row(gain):
    return gain[...].astype(F32).reshape(1, gain.shape[0])


def project(normed, columns):
    qkv = dot(normed, columns)
    half = columns.shape[1] // 3
    scale = (2 * half // HEADS) ** (-0.5)
    return qkv[:, :half].astype(BF) * BF(scale), qkv[:, half:].astype(BF)


def stack_heads(rows):
    lane = lax.broadcasted_iota(jnp.int32, rows.shape, 1)
    first = lane < rows.shape[1] // 2
    zero = jnp.zeros_like(rows)
    return jnp.concatenate([jnp.where(first, rows, zero), jnp.where(first, zero, rows)], axis=0)


def unstack_heads(stacked):
    rows = stacked.shape[0] // 2
    lane = lax.broadcasted_iota(jnp.int32, (rows, stacked.shape[1]), 1)
    return jnp.where(lane < stacked.shape[1] // 2, stacked[:rows], stacked[rows:])


def listed_balls(ball, mine, other, core):
    local_balls = mine.shape[1]
    lists, row = (mine, ball) if ball < local_balls else (other, ball - local_balls)
    return [lax.rem(lists[0, row, j] + core * local_balls, 2 * local_balls) for j in range(LISTED)]


def pick(ref, listed, first, half):
    return jnp.concatenate([ref[part_of(i, BALL), first : first + half] for i in listed], axis=0)


def turn_balls(turned_ref, kv_ref):
    for ball in range(turned_ref.shape[0]):
        turned_ref[ball] = kv_ref[ball * BALL : (ball + 1) * BALL, :].T


def pick_turned(ref, listed, first, half):
    return jnp.concatenate([ref[i, first : first + half, :] for i in listed], axis=1)


def combine(turned, weights):
    both = dot(turned, weights, ((1,), (1,)))
    rows, features = both.shape[1] // 2, both.shape[0] // 2
    return jnp.concatenate([both[:features, :rows], both[features:, rows:]], axis=0).T


def in_stages(count, *stages):
    held = {}
    for step in range(count + len(stages) - 1):
        for depth, stage in enumerate(stages):
            ball = step - depth
            if 0 <= ball < count:
                held[ball] = stage(ball, *held.pop(ball, ()))


def softmax_parts(scores):
    exponent = jnp.exp(scores - jnp.max(scores, axis=-1, keepdims=True))
    return exponent, 1.0 / jnp.sum(exponent, axis=-1, keepdims=True)


def forward_stages(lists, core, q_ref, kv_ref, attention_ref, mixed_ref):
    half = q_ref.shape[1]

    def products(ball):
        listed = listed_balls(ball, *lists, core)
        stacked = stack_heads(q_ref[ball * BALL : (ball + 1) * BALL, :])
        return listed, dot(stacked, pick(kv_ref, listed, 0, half), ((1,), (1,)))

    def elements(ball, listed, scores):
        exponent, inverse = softmax_parts(scores)
        attention = (exponent * inverse).astype(BF)
        attention_ref[ball] = attention
        return listed, attention

    def outputs(ball, listed, attention):
        mixed = unstack_heads(dot(attention, pick(kv_ref, listed, half, half)))
        mixed_ref[ball * BALL : (ball + 1) * BALL, :] = mixed.astype(BF)
        return ()

    return products, elements, outputs


def backward_stages(
    lists, core, q_ref, kv_ref, turned_ref, mg_ref, mixed_ref, grads_ref, dk_ref, dv_ref, attention_ref
):
    half = q_ref.shape[1]
    scale = (half // 2) ** (-0.5)

    def products(ball):
        listed = listed_balls(ball, *lists, core)
        grad = stack_heads(mg_ref[ball * BALL : (ball + 1) * BALL, :])
        return listed, grad, dot(grad, pick(kv_ref, listed, half, half), ((1,), (1,)))

    def elements(ball, listed, grad, weights_grad):
        mixed = mixed_ref[ball * BALL : (ball + 1) * BALL, :].astype(F32)
        inner = jnp.sum(grad.astype(F32) * jnp.concatenate([mixed, mixed], axis=0), axis=-1, keepdims=True)
        attention = attention_ref[ball]
        return listed, grad, attention, (attention.astype(F32) * (weights_grad - inner)).astype(BF)

    def gradients(ball, listed, grad, attention, scores_grad):
        at = slice(ball * BALL, (ball + 1) * BALL)
        queries_grad = combine(pick_turned(turned_ref, listed, 0, half), scores_grad) * scale
        grads_ref[at, :half] = queries_grad.astype(BF)
        add_listed(dk_ref, listed, dot(stack_heads(q_ref[at, :]), scores_grad, ((0,), (0,))))
        add_listed(dv_ref, listed, dot(grad, attention, ((0,), (0,))))
        return ()

    turn_balls(turned_ref, kv_ref)
    dk_ref[...] = jnp.zeros_like(dk_ref)
    dv_ref[...] = jnp.zeros_like(dv_ref)
    return products, elements, gradients


def add_listed(ref, listed, part):
    for j, i in enumerate(listed):
        ref[i] += part[:, j * BALL : (j + 1) * BALL]


def normed_grads(grads_ref, dk_ref, dv_ref, columns, store):
    half = dk_ref.shape[1]

    def turn(chunk):
        for ball in range(chunk * CHUNK // BALL, (chunk + 1) * CHUNK // BALL):
            at = slice(ball * BALL, (ball + 1) * BALL)
            grads_ref[at, half : 2 * half] = dk_ref[ball].T.astype(BF)
            grads_ref[at, 2 * half :] = dv_ref[ball].T.astype(BF)
        return ()

    def multiply(chunk):
        at = slice(chunk * CHUNK, (chunk + 1) * CHUNK)
        store(at, dot(grads_ref[at, :], columns, ((1,), (1,))))
        return ()

    in_stages(grads_ref.shape[0] // CHUNK, turn, multiply)


def geo_bit(bit):
    return lax.rem(lax.axis_index("geo") // bit, 2)


def kept(side, quartered):
    half = geo_bit(jnp.where(side == 0, 2, 1))
    return half, geo_bit(jnp.where(side == 0, 1, 2)) if quartered else 0


def store_quarters(ref, blocks, slot):
    size = ref.shape[1]
    ref[slot] = blocks[:size]
    ref[1 - slot] = blocks[size:]


def weight_part(part, normed_ref, grads, mixed, grad_out_ref):
    half = mixed.shape[1]
    weight = dot(normed_ref[:, part_of(part, half)], grads, ((0,), (0,)))
    out = dot(mixed, grad_out_ref[:, part_of(part, half)], ((0,), (0,)))
    blocks = [weight[:, i * half : (i + 1) * half] for i in range(3)] + [out]
    return jnp.concatenate(blocks, axis=0).astype(BF)


def norm_backward(normed_grad, x, gain, grad_out):
    factor = norm_factor(x)
    scaled = normed_grad.astype(BF).astype(F32) * gain
    inner = jnp.mean(scaled * x, axis=-1, keepdims=True)
    return (grad_out.astype(F32) + factor * scaled - x * (factor * factor * factor) * inner).astype(BF)


def norm_project(rows_count, rows_of, gain, columns, normed_ref, q_ref, kv_ref, first=0):
    def norm(chunk, x):
        return ((x * norm_factor(x) * gain).astype(BF),)

    def store(chunk, normed):
        at = slice(first + chunk * CHUNK, first + (chunk + 1) * CHUNK)
        normed_ref[at], (q_ref[at], kv_ref[at]) = normed, project(normed, columns)
        return ()

    in_stages(rows_count // CHUNK, lambda chunk: (rows_of(slice(chunk * CHUNK, (chunk + 1) * CHUNK)),), norm, store)


def project_mine(
    x_hbm, grad_hbm, rot_hbm, lists_one_hbm, lists_two_hbm, gain_one_hbm, gain_two_hbm, qkv_one_hbm, qkv_two_hbm, out_one_hbm, out_two_hbm,
    x, grad, rot, lists_one, lists_two, gain_one, gain_two, qkv_one, qkv_two, out_one, out_two,
    normed_ref, q_ref, kv_ref, sems,
):
    side = own_side()
    half = x.shape[1] // 2
    copies = []

    def start(source, target):
        copies.append(pltpu.make_async_copy(source, target, sems.at[len(copies)]))
        copies[-1].start()

    def start_columns(source, target):
        for i in range(3):
            start(source.at[:, part_of(2 * i + side, half)], target.at[:, i * half : (i + 1) * half])

    start(x_hbm, x)
    start(gain_one_hbm, gain_one)
    start_columns(qkv_one_hbm, qkv_one)
    first = len(copies)
    start(grad_hbm, grad)
    start(rot_hbm, rot)
    start(lists_one_hbm, lists_one)
    start(lists_two_hbm, lists_two)
    start(gain_two_hbm, gain_two)
    start_columns(qkv_two_hbm, qkv_two)
    for source, target in ((out_one_hbm, out_one), (out_two_hbm, out_two)):
        start(source.at[part_of(side, half)], target.at[:half])
        start(source.at[part_of(1 - side, half)], target.at[half:])
    for copy in copies[:first]:
        copy.wait()
    norm_project(
        x.shape[0], lambda at: x[at].astype(F32), gain_row(gain_one), qkv_one[...], normed_ref, q_ref, kv_ref
    )
    for copy in copies[first:]:
        copy.wait()


def first_forward(
    mine, other, x_other, gain, columns, normed_mine, q_mine, kv_mine, mixed_ref, q_ref, kv_ref, normed_ref,
    attention_ref,
):
    core = lax.axis_index("pts")
    local, width = x_other.shape
    half = width // 2
    normed_ref[:local], q_ref[:local], kv_ref[:local] = normed_mine[...], q_mine[...], kv_mine[...]
    norm_project(
        local, lambda at: x_other[at].astype(F32), gain_row(gain), columns[...], normed_ref, q_ref, kv_ref, local
    )
    stages = forward_stages((mine, other), core, q_ref, kv_ref, attention_ref, mixed_ref)
    in_stages(2 * local // BALL, *stages)


def before_second(
    rot_mine, rot_other, x_mine, x_other, mixed, grad_mine, grad_other, out_one, out_two,
    base_ref, chosen_ref, chosen_back, grad_ref, mg_ref,
):
    core = lax.axis_index("pts")
    local, width = x_mine.shape
    half = width // 2
    total = 2 * local
    own = out_one[:half]
    base_ref[:local] = x_mine[...].astype(F32) + dot(mixed[:local], own)
    base_ref[local:] = x_other[...].astype(F32) + dot(mixed[local:], own)
    grad_ref[:local] = grad_mine[...]
    grad_ref[local:] = grad_other[...]
    mg_ref[...] = dot(grad_ref[...], out_two[:half], ((1,), (1,))).astype(BF)
    lane = lax.broadcasted_iota(jnp.int32, (BALL, total), 1)
    lane = lax.rem(lane + core * local, total).astype(F32)
    for side, ref in enumerate((rot_mine, rot_other)):
        for j in range(local // BALL):
            row = ref[j : j + 1, :].astype(F32)
            column = jnp.broadcast_to(row, (BALL, BALL)).T[:, :1]
            first = side * local + j * BALL
            chosen_ref[first : first + BALL, :] = (lane == column).astype(BF)
    row_of = [ref[j : j + 1, :] for ref in (rot_mine, rot_other) for j in range(local // BALL)]
    order = lax.rem(jnp.concatenate(row_of, axis=1) + core * local, total)
    place = lax.broadcasted_iota(jnp.int32, (BALL, total), 0)
    for first in range(0, total, BALL):
        chosen_back[first : first + BALL, :] = (place == order - first).astype(BF)


def second_layer(
    mine, other, base, mixed_other, chosen, mg_ref, out_one, gain, columns,
    moved_ref, normed_ref, mixed_ref, mixed_send, grads_ref, part_ref,
    hidden_ref, q_ref, kv_ref, turned_ref, attention_ref, dk_ref, dv_ref,
):
    core = lax.axis_index("pts")
    total, width = base.shape
    local = total // 2
    half = width // 2
    far = out_one[half:]
    for first in range(0, total, CHUNK):
        other_first = (first + local) % total
        added = dot(mixed_other[other_first : other_first + CHUNK], far)
        hidden_ref[first : first + CHUNK] = (base[first : first + CHUNK] + added).astype(BF)

    def rotate(at):
        moved = dot(chosen[at], hidden_ref[...])
        moved_ref[at] = moved.astype(BF)
        return moved

    norm_project(total, rotate, gain_row(gain), columns[...], normed_ref, q_ref, kv_ref)
    lists = (mine, other)
    forward = forward_stages(lists, core, q_ref, kv_ref, attention_ref, mixed_ref)
    backward = backward_stages(
        lists, core, q_ref, kv_ref, turned_ref, mg_ref, mixed_ref, grads_ref, dk_ref, dv_ref, attention_ref
    )
    in_stages(total // BALL, *forward, *backward)

    def store(at, part):
        part_ref[at] = part.astype(BF)

    normed_grads(grads_ref, dk_ref, dv_ref, columns[...], store)
    mixed_send[...] = mixed_ref[local:]


def second_weights(normed, grads, mixed, grad, keep_ref, send_ref):
    part, slot = kept(own_side(), QUARTERED[1])
    store_quarters(send_ref, weight_part(1 - part, normed, grads[...], mixed[...], grad), slot)
    store_quarters(keep_ref, weight_part(part, normed, grads[...], mixed[...], grad), slot)


def first_backward(
    mine, other, chosen_back, part_mine, part_other, moved, grad, gain_two,
    mixed_ref, normed, q_ref, kv_ref, attention_ref, out_one, columns,
    hg_ref, grads_ref, send_ref, part_keep, part_send,
    rows_grad_ref, mg_ref, turned_ref, dk_ref, dv_ref,
):
    core = lax.axis_index("pts")
    total, width = grad.shape
    local = total // 2
    half = width // 2
    gain = gain_row(gain_two)
    for first, far in ((0, local), (local, 0)):
        at = slice(first, first + local)
        normed_grad = part_mine[at].astype(F32) + part_other[far : far + local].astype(F32)
        rows_grad_ref[at] = norm_backward(normed_grad, moved[at].astype(F32), gain, grad[at])

    def rotate(chunk):
        return (dot(chosen_back[chunk * CHUNK : (chunk + 1) * CHUNK], rows_grad_ref[...]).astype(BF),)

    def project_back(chunk, hidden_grad):
        at = slice(chunk * CHUNK, (chunk + 1) * CHUNK)
        hg_ref[at] = hidden_grad
        mg_ref[at] = dot(hidden_grad, out_one[:half], ((1,), (1,))).astype(BF)
        return ()

    stages = backward_stages(
        (mine, other), core, q_ref, kv_ref, turned_ref, mg_ref, mixed_ref, grads_ref, dk_ref, dv_ref, attention_ref
    )
    in_stages(total // CHUNK, rotate, project_back)
    in_stages(total // BALL, *stages)

    def store(at, part):
        if at.start < local:
            part_keep[at] = part
        else:
            part_send[at.start - local : at.stop - local] = part.astype(BF)

    normed_grads(grads_ref, dk_ref, dv_ref, columns[...], store)
    part, slot = kept(own_side(), QUARTERED[0])
    store_quarters(send_ref, weight_part(1 - part, normed, grads_ref[...], mixed_ref[...], hg_ref), slot)


def finish_rows(
    normed, grads, mixed, hidden_grad, part_mine, part_other, x_mine, gain, moved, mixed_two, mixed_two_other, out_two,
    keep_ref, points_grad, result,
):
    local = x_mine.shape[0]
    part, slot = kept(own_side(), QUARTERED[0])
    store_quarters(keep_ref, weight_part(part, normed, grads[...], mixed[...], hidden_grad), slot)
    normed_grad = part_mine[...] + part_other[...].astype(F32)
    points_grad[...] = norm_backward(
        normed_grad, x_mine[...].astype(F32), gain_row(gain), hidden_grad[:local]
    )
    both = jnp.concatenate([mixed_two[:local], mixed_two_other[...]], axis=1)
    result[...] = (moved[:local].astype(F32) + dot(both, out_two[...])).astype(BF)


def finish_weights(
    quartered, near_mine, far_mine, near_other, far_other, gain, weight, gain_grad, qkv_grad, out_grad, folded_ref
):
    own = own_side()
    size, half = near_mine.shape[1:]
    for side, near, far in ((own, near_mine, far_mine), (1 - own, near_other, far_other)):
        bit, slot = kept(side, quartered)
        for part, ref in ((bit, near), (1 - bit, far)):

            def block(p):
                first = p * half
                quarter = slot if first < size else 1 - slot
                return ref[quarter, first % size : first % size + half].astype(F32)

            at = part_of(part, half)
            folded = jnp.zeros((half, half), F32)
            for p in range(3):
                columns = part_of(2 * p + side, half)
                qkv_grad[at, columns] = block(p)
                folded = folded + block(p) * weight[at, columns].astype(F32)
            folded_ref[side, at] = folded
            out_grad[part_of(side, half), at] = block(3)
    folded = folded_ref[0] + folded_ref[1]
    gain_grad[...] = jnp.sum(folded.T, axis=0, keepdims=True) / gain_row(gain)


def shape(*dims, dtype=BF):
    return jax.ShapeDtypeStruct(dims, dtype)


def call(body, ins, outs, scratch=(), lists=()):
    return pl.pallas_call(
        body,
        name=getattr(body, "func", body).__name__,
        out_shape=outs,
        in_specs=[SMEM] * len(lists) + [VMEM] * len(ins),
        out_specs=[VMEM] * len(outs),
        scratch_shapes=[pltpu.VMEM(item.shape, item.dtype) for item in scratch],
        compiler_params=PARAMS,
    )(*lists, *ins)


def add(a, b):
    return (a.astype(F32) + b.astype(F32)).astype(BF)


def local(
    geo,
    points,
    result_grad,
    lists_one,
    lists_two,
    rotation,
    gain_one,
    qkv_one,
    out_one,
    gain_two,
    qkv_two,
    out_two,
):
    rows, width = points.shape[1:]
    half = width // 2
    total = 2 * rows
    balls = total // BALL
    thin, wide, triple = shape(total, half), shape(total, width), shape(total, 3 * half)
    turned = shape(balls, width, BALL)
    kept_attention = shape(balls, 2 * BALL, LISTED * BALL)
    blocks = shape(balls, half, BALL, dtype=F32)
    weights = shape(2, width, half)

    def swap(array):
        return lax.ppermute(array, "pts", SWAP)

    def across(array, bits):
        def place(side, index):
            return (side ^ parity(index)) * geo + index

        pairs = [(place(side, i), place(side, i ^ bit)) for side, bit in enumerate(bits) for i in range(geo)]
        return lax.ppermute(array, ("pts", "geo"), pairs)

    ups = [1 << i for i in range(2, geo.bit_length() - 1)]
    doublings = [(1, 2)] + list(zip(ups, ups[1:] + ups[:1]))

    x = points[0]
    grad = result_grad[0]
    rot = rotation.reshape(rows // BALL, BALL)
    others = [swap(a) for a in (x, lists_one, lists_two, rot, grad)]
    arguments = (x, grad, rot, lists_one, lists_two, gain_one, gain_two, qkv_one, qkv_two, out_one, out_two)
    own_rows = shape(rows, width)
    own_columns = shape(width, 3 * half)
    square = shape(width, width)
    x, grad, rot, *mine, near_gain, far_gain, columns_one, columns_two, out_one, out_two, normed, q, kv = pl.pallas_call(
        project_mine,
        name="project_mine",
        out_shape=[shape(*a.shape, dtype=a.dtype) for a in arguments[:7]]
        + [own_columns, own_columns, square, square, own_rows, shape(rows, half), own_rows],
        in_specs=[HBM] * len(arguments),
        out_specs=[VMEM] * 14,
        scratch_shapes=[pltpu.SemaphoreType.DMA((17,))],
        compiler_params=PARAMS,
    )(*[pltpu.with_memory_space_constraint(a, pltpu.HBM) for a in arguments])
    x_other, one_other, two_other, rot_other, grad_other = lax.optimization_barrier(others)
    one = [mine[0], one_other]
    two = [mine[1], two_other]
    mixed, q, kv, normed, attention = call(
        first_forward, [x_other, near_gain, columns_one, normed, q, kv], [thin, thin, wide, wide, kept_attention], lists=one
    )
    mixed_other = swap(mixed)
    base, chosen, chosen_back, grads_in, mg = call(
        before_second,
        [rot, rot_other, x, x_other, mixed, grad, grad_other, out_one, out_two],
        [shape(total, width, dtype=F32), shape(total, total), shape(total, total), wide, thin],
    )
    moved, normed_two, mixed_two, mixed_send, grads_two, part_two = call(
        second_layer,
        [base, mixed_other, chosen, mg, out_one, far_gain, columns_two],
        [wide, wide, thin, shape(rows, half), triple, wide],
        [wide, thin, wide, turned, kept_attention, blocks, blocks],
        two,
    )
    part_two_other = swap(part_two)
    mixed_two_other = swap(mixed_send)
    keep_two, send_two = call(second_weights, [normed_two, grads_two, mixed_two, grads_in], [weights, weights])
    received_two = across(send_two, (2, 1))
    hidden_grad, grads_one, send, part_keep, part_send = call(
        first_backward,
        [chosen_back, part_two, part_two_other, moved, grads_in, far_gain, mixed, normed, q, kv, attention]
        + [out_one, columns_one],
        [wide, triple, weights, shape(rows, width, dtype=F32), own_rows],
        [wide, thin, turned, blocks, blocks],
        one,
    )
    received_two, send = lax.optimization_barrier((received_two, send))
    summed_two = add(keep_two, received_two)
    part_other = swap(part_send)
    received = across(send, (2, 1))
    keep, points_grad, result = call(
        finish_rows,
        [normed, grads_one, mixed, hidden_grad, part_keep, part_other, x, near_gain]
        + [moved, mixed_two, mixed_two_other, out_two],
        [weights, own_rows, own_rows],
    )
    summed = add(keep, received)

    first, rest = doublings[0], doublings[1:]

    def second_step(array, quartered):
        return add(array[:1], across(array[1:], first)) if quartered else add(array, across(array, first))

    summed_two = second_step(summed_two, QUARTERED[1])
    summed = second_step(summed, QUARTERED[0])
    for bits in rest:
        summed_two = add(summed_two, across(summed_two, bits))
        summed = add(summed, across(summed, bits))

    def widen(array, quartered):
        return jnp.concatenate([array, across(array, first)], axis=0) if quartered else array

    summed_two = widen(summed_two, QUARTERED[1])
    summed = widen(summed, QUARTERED[0])
    far_two = across(summed_two, (2, 1))
    far = across(summed, (2, 1))
    tied_two, tied_far_two, _ = lax.optimization_barrier((summed_two, far_two, summed))
    pieces_two = [summed_two, far_two, swap(tied_two), swap(tied_far_two)]
    pieces_one = [summed, far, swap(summed), swap(far)]
    grads = []
    for quartered, pieces, gain, weight in (
        (QUARTERED[0], pieces_one, near_gain, qkv_one),
        (QUARTERED[1], pieces_two, far_gain, qkv_two),
    ):
        found = call(
            functools.partial(finish_weights, quartered),
            pieces + [gain, weight],
            [shape(*dims, dtype=F32) for dims in ((1, width), (width, 3 * width), (width, width))],
            [shape(2, width, half, dtype=F32)],
        )
        grads += [found[0].reshape(width), found[1], found[2]]
    return (result[None], points_grad[None], *grads)


def solution(mesh):
    rows = P("geo", "pts", None)
    placed = (rows,) * 4 + (P("geo", "pts"),) + (P(),) * 6
    return jax.shard_map(
        functools.partial(local, mesh.shape["geo"]),
        mesh=mesh,
        in_specs=placed,
        out_specs=(rows, rows) + (P(),) * 6,
        check_vma=False,
    )
```
